256 devices in a mesh: ctx: 64 (over x, z, core), tp: 4 (over y).
Axes of the slice: x: 4, y: 4, z: 8, core: 2. Of those that a mesh axis runs over, the one named last changes fastest.
Arguments:
- tokens: bfloat16 [16384, 7168], P('ctx', 'tp'), may hold values from -6 to 6
- router_weight: bfloat16 [7168], P('tp'), may hold values from -0.0625 to 0.0625
- queries: bfloat16 [16384, 3584], P('ctx', 'tp'), may hold values from -48 to 48
- keys_values: bfloat16 [16384, 2, 512], P('ctx', None, 'tp'), may hold values from -12 to 12
- routed_grad: bfloat16 [16384, 3584], P('ctx', 'tp'), may hold values from -6 to 6
- chosen: int32 [64, 64], P('ctx'), may hold values from 0 to 255, as said below
- counts: int32 [64], replicated, may hold values from 1 to 64, 2048 in all
Outputs:
- routed: bfloat16 [16384, 3584], P('ctx', 'tp')
- d_queries: bfloat16 [16384, 3584], P('ctx', 'tp')
- key_value_gradient: bfloat16 [16384, 2, 512], P('ctx', None, 'tp')
- router_grad: float32 [7168], P('tp')
The draws below stay inside these ranges and needn't reach their ends.
Inputs may be any that keep to these rules, and one draw needn't show every extreme that they name: `chosen`: row c holds 64 distinct positions of shard c in increasing order; its first counts[c] entries are the routed tokens. The counts sum to 2048; the largest equals 64.
All inputs are finite; a program needn't handle non-finite values.
Results may differ from the reference program's by a relative error of at most 0.011.
Values may be sent and summed in bfloat16 or wider, within the bound.
No kernel may reach another device: no remote copies, remote signals or barrier semaphores. Data moves between devices by JAX's collectives and lax.ppermute only.
A program may use at most 64 MiB of HBM per device.

```python
import math
import jax
import jax.numpy as jnp
import numpy as np
from jax import lax

D = 7168
QUERY_HEADS = 28
KEY_VALUE_HEADS = 4
HEAD_SIZE = 128
TOK_DEV = 256
PER = 32
CAP = 64
CHOSEN_TOTAL = 2048
SEQUENCE_TOKENS = 16384
N_CTX = 64


def draw_queries(key, part):
    key = jax.random.fold_in(key, 21)
    random_noise_key = jax.random.fold_in(key, 0)
    sampled_input = jnp.clip(jax.random.normal(random_noise_key, (SEQUENCE_TOKENS, QUERY_HEADS, HEAD_SIZE), jnp.float32), -6.0, 6.0)
    return sampled_input.reshape(SEQUENCE_TOKENS, QUERY_HEADS * HEAD_SIZE).astype(jnp.bfloat16)


def draw_keys_values(key, part):
    key = jax.random.fold_in(key, 22)
    random_noise_key = jax.random.fold_in(key, 0)
    sampled_input = jnp.clip(jax.random.normal(random_noise_key, (SEQUENCE_TOKENS, 2, KEY_VALUE_HEADS, HEAD_SIZE), jnp.float32), -6.0, 6.0)
    return sampled_input.reshape(SEQUENCE_TOKENS, 2, KEY_VALUE_HEADS * HEAD_SIZE).astype(jnp.bfloat16)


def draw_chosen(key, part):
    key = jax.random.fold_in(key, 23)

    def one_shard(shard_key):
        shuffled = jax.random.permutation(shard_key, TOK_DEV)
        return jnp.nonzero(shuffled < CAP, size=CAP)[0].astype(jnp.int32)
    return jax.vmap(one_shard)(jax.random.split(key, N_CTX))


def shard_levels(own_key, shape, cuts, least, largest):
    def one(dim, blocks):
        steps = jax.random.uniform(jax.random.fold_in(jax.random.fold_in(own_key, 6), dim), (blocks,), jnp.float32, least / len(cuts), largest / len(cuts))
        return jnp.repeat(jnp.exp(steps), shape[dim] // blocks).reshape((-1,) + (1,) * (len(shape) - dim - 1))

    loudness = one(*cuts[0])
    for cut in cuts[1:]:
        loudness = loudness * one(*cut)
    return loudness


def length_profile(number_of, total, bound, skew):
    weights = [(1 << 20) // math.isqrt(rank ** skew) + 1 for rank in range(2, number_of + 1)]
    rest, given = total - bound - (number_of - 1), [1] * (number_of - 1)
    while rest > 0:
        free = [i for i in range(number_of - 1) if given[i] < bound]
        whole, left = sum([weights[i] for i in free]), rest
        for i in free:
            more = min(bound - given[i], max(1, left * weights[i] // whole), rest)
            given[i] = given[i] + more
            rest = rest - more
    return np.array([bound] + given)


def ragged(stream_key, count, total, limit, slope):
    if count == 2:
        one = jax.random.randint(stream_key, (), max(1, total - limit), min(limit, total - 1) + 1)
        return jnp.stack([one, total - one])
    tallies = jnp.asarray(length_profile(count, total, limit, slope), jnp.int32)
    pairs = (count - 1) // 2
    giver, receiver = tallies[1:1 + 2 * pairs:2], tallies[2:2 + 2 * pairs:2]
    room = jnp.minimum(giver - 1, limit - receiver)
    passed = jax.random.randint(jax.random.fold_in(stream_key, 1), (pairs,), 0, 1 << 20) % (room + 1)
    tallies = tallies.at[1:1 + 2 * pairs:2].set(giver - passed).at[2:2 + 2 * pairs:2].set(receiver + passed)
    return tallies[jax.random.permutation(jax.random.fold_in(stream_key, 2), count)]


def gaussian(rng, dims, deviation, most, cuts=(), held_as=jnp.bfloat16):
    level = shard_levels(rng, dims, cuts, -0.22, 0.18) if cuts else 1.0
    drawn = jax.random.normal(rng, dims, jnp.float32) * deviation * level
    return jnp.minimum(jnp.maximum(drawn, -most), most).astype(held_as)


def setup_inputs(seed: int = 0) -> dict:
    seeds = jax.random.split(jax.random.key(seed), 8)
    return {
        "tokens": gaussian(seeds[0], (SEQUENCE_TOKENS, D), 1.0, 6.0, ((0, 64), (1, 4))),
        "router_weight": gaussian(seeds[1], (D,), D ** -0.5, 0.0625, ((0, 4),)),
        "queries": draw_queries(jax.random.fold_in(seeds[7], 71), 0),
        "keys_values": draw_keys_values(jax.random.fold_in(seeds[7], 71), 0),
        "routed_grad": gaussian(seeds[4], (SEQUENCE_TOKENS, QUERY_HEADS * HEAD_SIZE), 1.0, 6.0, ((0, 64), (1, 4))),
        "chosen": draw_chosen(jax.random.fold_in(seeds[7], 71), 0),
        "counts": ragged(seeds[6], N_CTX, PER * N_CTX, CAP, 2).astype(jnp.int32),
    }


def reference(tokens, router_weight, queries, keys_values, routed_grad, chosen, counts):
    slot_ids = jnp.arange(CAP, dtype=jnp.int32)
    offsets = (jnp.cumsum(counts) - counts).astype(jnp.int32)
    is_live = slot_ids[None, :] < counts[:, None]
    ranking = offsets[:, None] + slot_ids[None, :]
    position = jnp.arange(N_CTX, dtype=jnp.int32)[:, None] * TOK_DEV + chosen
    target = jnp.where(is_live, ranking, CHOSEN_TOTAL).reshape(-1).astype(jnp.int32)
    selected_tokens = jnp.zeros((CHOSEN_TOTAL,), jnp.int32).at[target].set(position.reshape(-1).astype(jnp.int32), mode="drop")
    feature_rows = tokens[selected_tokens]
    logits = jnp.dot(feature_rows, router_weight, preferred_element_type=jnp.float32)
    gate_value = jax.nn.sigmoid(logits)
    query_group_width = QUERY_HEADS // KEY_VALUE_HEADS
    scale_value = HEAD_SIZE ** -0.5
    query_heads = queries[selected_tokens].reshape(CHOSEN_TOTAL, QUERY_HEADS, HEAD_SIZE).transpose(1, 0, 2)
    key_value_rows = keys_values[selected_tokens]
    key_head_rows = key_value_rows[:, 0].reshape(CHOSEN_TOTAL, KEY_VALUE_HEADS, HEAD_SIZE).transpose(1, 0, 2)
    value_head_rows = key_value_rows[:, 1].reshape(CHOSEN_TOTAL, KEY_VALUE_HEADS, HEAD_SIZE).transpose(1, 0, 2)
    kv_of_head = jnp.arange(QUERY_HEADS, dtype=jnp.int32) // query_group_width
    order_ids = jnp.arange(CHOSEN_TOTAL, dtype=jnp.int32)
    causal = order_ids[:, None] >= order_ids[None, :]

    def head_probs(query, key_rows):
        scores = jnp.dot(query, key_rows.T, preferred_element_type=jnp.float32) * scale_value
        scores = jnp.where(causal, scores, -jnp.inf)
        weights = jnp.exp(scores - jnp.max(scores, axis=1, keepdims=True))
        return weights / jnp.sum(weights, axis=1, keepdims=True)

    def forward_head(inputs):
        query, kv_index = inputs
        probs = head_probs(query, key_head_rows[kv_index])
        mixture = jnp.dot(probs.astype(jnp.bfloat16), value_head_rows[kv_index], preferred_element_type=jnp.float32)
        return mixture.astype(jnp.bfloat16)

    attended = lax.map(forward_head, (query_heads, kv_of_head))
    attended = attended.transpose(1, 0, 2).reshape(CHOSEN_TOTAL, QUERY_HEADS * HEAD_SIZE)
    routed_rows = (gate_value[:, None] * attended.astype(jnp.float32)).astype(jnp.bfloat16)
    routed = jnp.zeros((SEQUENCE_TOKENS, QUERY_HEADS * HEAD_SIZE), jnp.bfloat16).at[selected_tokens].set(routed_rows)
    grad_rows = routed_grad[selected_tokens].astype(jnp.float32)
    d_gate = jnp.sum(grad_rows * attended.astype(jnp.float32), axis=1)
    d_attended = (gate_value[:, None] * grad_rows).astype(jnp.bfloat16)
    d_logit = d_gate * gate_value * (1.0 - gate_value)
    router_grad = jnp.sum(feature_rows.astype(jnp.float32) * d_logit[:, None], axis=0)
    d_heads = d_attended.reshape(CHOSEN_TOTAL, QUERY_HEADS, HEAD_SIZE).transpose(1, 0, 2)

    def backward_head(inputs):
        query, d_rows, kv_index = inputs
        key_rows = key_head_rows[kv_index]
        value_rows = value_head_rows[kv_index]
        probs = head_probs(query, key_rows)
        weights_low = probs.astype(jnp.bfloat16)
        value_gradient = jnp.dot(weights_low.T, d_rows, preferred_element_type=jnp.float32)
        d_probs = jnp.dot(d_rows, value_rows.T, preferred_element_type=jnp.float32)
        row_delta = jnp.sum(probs * d_probs, axis=1, keepdims=True)
        d_scores = (probs * (d_probs - row_delta)).astype(jnp.bfloat16)
        d_query = (jnp.dot(d_scores, key_rows, preferred_element_type=jnp.float32) * scale_value).astype(jnp.bfloat16)
        key_gradient = jnp.dot(d_scores.T, query, preferred_element_type=jnp.float32) * scale_value
        return d_query, key_gradient, value_gradient

    d_query, key_gradient, value_gradient = lax.map(backward_head, (query_heads, d_heads, kv_of_head))
    d_query = d_query.transpose(1, 0, 2).reshape(CHOSEN_TOTAL, QUERY_HEADS * HEAD_SIZE)
    key_gradient = key_gradient.reshape(KEY_VALUE_HEADS, query_group_width, CHOSEN_TOTAL, HEAD_SIZE).sum(axis=1).transpose(1, 0, 2).reshape(CHOSEN_TOTAL, KEY_VALUE_HEADS * HEAD_SIZE)
    value_gradient = value_gradient.reshape(KEY_VALUE_HEADS, query_group_width, CHOSEN_TOTAL, HEAD_SIZE).sum(axis=1).transpose(1, 0, 2).reshape(CHOSEN_TOTAL, KEY_VALUE_HEADS * HEAD_SIZE)
    pair_gradients = jnp.stack((key_gradient, value_gradient), axis=1).astype(jnp.bfloat16)
    d_queries = jnp.zeros((SEQUENCE_TOKENS, QUERY_HEADS * HEAD_SIZE), jnp.bfloat16).at[selected_tokens].set(d_query)
    key_value_gradient = jnp.zeros((SEQUENCE_TOKENS, 2, KEY_VALUE_HEADS * HEAD_SIZE), jnp.bfloat16).at[selected_tokens].set(pair_gradients)
    return routed, d_queries, key_value_gradient, router_grad
```

```python
import jax
import jax.numpy as jnp
from jax import lax
from jax.sharding import PartitionSpec as P

HEAD_SIZE = 128
NX, NZ = 4, 8


def shard_of(x, z, c):
    return (x * NZ + z) * 2 + c


def move(value, target):
    pairs = [
        (shard_of(x, z, c), shard_of(*target(x, z, c)))
        for x in range(NX)
        for z in range(NZ)
        for c in range(2)
    ]
    return lax.ppermute(value, "ctx", pairs)


def by_x(k):
    return lambda x, z, c: ((x + k) % NX, z, c)


def by_z(k):
    return lambda x, z, c: (x, (z + k) % NZ, c)


def flip_z(x, z, c):
    return (x, z ^ 1, c)


def flip_core(x, z, c):
    return (x, z, c ^ 1)


def gather_shards(rows):
    rows = jnp.concatenate([rows, move(rows, flip_z)])
    rows = jnp.concatenate([rows] + [move(rows, by_z(k)) for k in (2, 4, 6)])
    rows = jnp.concatenate([rows] + [move(rows, by_x(k)) for k in (1, 2, 3)])
    return jnp.concatenate([rows, move(rows, flip_core)])


def block_shards(this_shard):
    core = this_shard % 2
    z = (this_shard // 2) % NZ
    x = this_shard // (2 * NZ)
    blocks = jnp.arange(2 * NX * NZ, dtype=jnp.int32)
    z_flip, z_shift, x_shift, core_flip = (
        blocks % 2,
        (blocks // 2) % 4,
        (blocks // 8) % 4,
        blocks // 32,
    )
    return shard_of(
        (x - x_shift + NX) % NX, ((z ^ z_flip) - 2 * z_shift + NZ) % NZ, core ^ core_flip
    )


def sum_parts(parts):
    total = parts[0].astype(jnp.float32)
    for part in parts[1:]:
        total = total + part.astype(jnp.float32)
    return total


def reduce_step(total, targets):
    low = total.astype(jnp.bfloat16)
    return sum_parts([total[0]] + [move(low[i + 1], t) for i, t in enumerate(targets)])


def reduce_shards(total):
    total = total.reshape(2, 4, 4, 2, -1, total.shape[-1])
    total = reduce_step(total, [flip_core])
    total = reduce_step(total, [by_x(-k) for k in (1, 2, 3)])
    total = reduce_step(total, [by_z(-k) for k in (2, 4, 6)])
    return reduce_step(total, [flip_z])


def sum_over_ctx(part):
    part = part + move(part, flip_core)
    part = part + sum_parts([move(part, by_x(k)) for k in (1, 2, 3)])
    part = part + move(part, flip_z)
    return part + sum_parts([move(part, by_z(k)) for k in (2, 4, 6)])


def score_block(query_block, key_rows, key_rank, key_valid, query_rank):
    scores = jnp.einsum(
        "bhgd,khd->hgbk", query_block, key_rows, preferred_element_type=jnp.float32
    ) * HEAD_SIZE ** (-0.5)
    allowed = key_valid[None, None, None, :] & (
        key_rank[None, None, None, :] <= query_rank[None, None, :, None]
    )
    return jnp.where(allowed, scores, -jnp.inf)


def split_blocks(query_rows, kv_heads):
    row_count = query_rows.shape[0]
    block_rows = min(row_count, 64)
    blocks = row_count // block_rows
    query_group_width = query_rows.shape[1] // (kv_heads * HEAD_SIZE)
    return (blocks, block_rows, query_group_width)


def attend_forward(query_rows, query_rank, key_rows, value_rows, key_rank, key_valid):
    kv_heads = key_rows.shape[1]
    blocks, block_rows, query_group_width = split_blocks(query_rows, kv_heads)
    query_blocks = query_rows.reshape(blocks, block_rows, kv_heads, query_group_width, HEAD_SIZE)
    rank_blocks = query_rank.reshape(blocks, block_rows)

    def forward_block(pieces):
        query_block, rank_block = pieces
        scores = score_block(query_block, key_rows, key_rank, key_valid, rank_block)
        row_max = jnp.max(scores, axis=-1, keepdims=True)
        weights = jnp.exp(scores - row_max)
        row_sum = jnp.sum(weights, axis=-1, keepdims=True)
        weights_low = (weights / row_sum).astype(jnp.bfloat16)
        mixture = jnp.einsum(
            "hgbk,khd->bhgd", weights_low, value_rows, preferred_element_type=jnp.float32
        )
        return (mixture.astype(jnp.bfloat16).reshape(block_rows, -1), row_max, row_sum)

    attended, row_maxes, row_sums = lax.map(forward_block, (query_blocks, rank_blocks))
    return (attended.reshape(query_rows.shape[0], -1), row_maxes, row_sums)


def attend_backward(
    query_rows, query_rank, d_rows, key_rows, value_rows, key_rank, key_valid, row_maxes, row_sums
):
    kv_heads = key_rows.shape[1]
    blocks, block_rows, query_group_width = split_blocks(query_rows, kv_heads)
    query_blocks = query_rows.reshape(blocks, block_rows, kv_heads, query_group_width, HEAD_SIZE)
    rank_blocks = query_rank.reshape(blocks, block_rows)
    d_blocks = d_rows.reshape(blocks, block_rows, kv_heads, query_group_width, HEAD_SIZE)
    scale_value = HEAD_SIZE ** (-0.5)

    def backward_block(totals, pieces):
        d_keys, d_values = totals
        query_block, rank_block, d_block, row_max, row_sum = pieces
        scores = score_block(query_block, key_rows, key_rank, key_valid, rank_block)
        probs = jnp.exp(scores - row_max) / row_sum
        weights_low = probs.astype(jnp.bfloat16)
        d_values = d_values + jnp.einsum(
            "hgbk,bhgd->khd", weights_low, d_block, preferred_element_type=jnp.float32
        )
        d_probs = jnp.einsum(
            "bhgd,khd->hgbk", d_block, value_rows, preferred_element_type=jnp.float32
        )
        row_delta = jnp.sum(probs * d_probs, axis=-1, keepdims=True)
        d_scores = (probs * (d_probs - row_delta)).astype(jnp.bfloat16)
        d_query = (
            jnp.einsum("hgbk,khd->bhgd", d_scores, key_rows, preferred_element_type=jnp.float32)
            * scale_value
        )
        d_keys = (
            d_keys
            + jnp.einsum(
                "hgbk,bhgd->khd", d_scores, query_block, preferred_element_type=jnp.float32
            )
            * scale_value
        )
        return ((d_keys, d_values), d_query.astype(jnp.bfloat16).reshape(block_rows, -1))

    empty = jnp.zeros(key_rows.shape, jnp.float32)
    (d_keys, d_values), d_queries = lax.scan(
        backward_block, (empty, empty), (query_blocks, rank_blocks, d_blocks, row_maxes, row_sums)
    )
    return (d_queries.reshape(query_rows.shape[0], -1), d_keys, d_values)


def split_pairs(all_pairs, kv_heads):
    key_count = all_pairs.shape[0]
    kv_width = kv_heads * HEAD_SIZE
    key_rows = all_pairs[:, :kv_width].reshape(key_count, kv_heads, HEAD_SIZE)
    value_rows = all_pairs[:, kv_width:].reshape(key_count, kv_heads, HEAD_SIZE)
    return (key_rows, value_rows)


def join_pairs(d_keys, d_values):
    key_count = d_keys.shape[0]
    return jnp.concatenate((d_keys.reshape(key_count, -1), d_values.reshape(key_count, -1)), axis=1)


def on_device(tokens, router_weight, queries, keys_values, routed_grad, chosen, counts):
    shards = lax.axis_size("ctx")
    this_shard = lax.axis_index("ctx")
    capacity = chosen.shape[1]
    local_rows = chosen[0]
    kv_heads = keys_values.shape[2] // HEAD_SIZE
    slot_ids = jnp.arange(capacity, dtype=jnp.int32)
    shard_ids = jnp.arange(shards, dtype=jnp.int32)
    offsets = jnp.cumsum(counts) - counts
    is_mine = shard_ids == this_shard
    my_offset = jnp.sum(jnp.where(is_mine, offsets, 0))
    my_count = jnp.sum(jnp.where(is_mine, counts, 0))
    is_live = slot_ids < my_count
    feature_rows = tokens[local_rows]
    logit_part = jnp.dot(feature_rows, router_weight, preferred_element_type=jnp.float32)
    logits = lax.psum(logit_part, "tp")
    gate_value = jax.nn.sigmoid(logits)
    query_rows = queries[local_rows]
    key_value_rows = keys_values[local_rows].reshape(capacity, -1)
    all_pairs = gather_shards(key_value_rows)
    block_ids = block_shards(this_shard)
    key_rows, value_rows = split_pairs(all_pairs, kv_heads)
    key_rank = (offsets[block_ids][:, None] + slot_ids[None, :]).reshape(-1)
    key_valid = (slot_ids[None, :] < counts[block_ids][:, None]).reshape(-1)
    query_rank = jnp.where(is_live, my_offset + slot_ids, 1 << 30)
    attended, row_maxes, row_sums = attend_forward(
        query_rows, query_rank, key_rows, value_rows, key_rank, key_valid
    )
    routed_rows = (gate_value[:, None] * attended.astype(jnp.float32)).astype(jnp.bfloat16)
    grad_rows = routed_grad[local_rows].astype(jnp.float32)
    gate_part = jnp.sum(grad_rows * attended.astype(jnp.float32), axis=1)
    d_gate = lax.psum(gate_part, "tp")
    d_attended = jnp.where(is_live[:, None], gate_value[:, None] * grad_rows, 0.0).astype(
        jnp.bfloat16
    )
    d_logit = jnp.where(is_live, d_gate * gate_value * (1.0 - gate_value), 0.0)
    routed_rows, d_attended, d_logit = (routed_rows, d_attended, d_logit)
    d_query, d_keys, d_values = attend_backward(
        query_rows,
        query_rank,
        d_attended,
        key_rows,
        value_rows,
        key_rank,
        key_valid,
        row_maxes,
        row_sums,
    )
    own_pairs = reduce_shards(join_pairs(d_keys, d_values)).astype(jnp.bfloat16)
    live_column = is_live[:, None]
    routed = (
        jnp.zeros(queries.shape, jnp.bfloat16)
        .at[local_rows]
        .set(jnp.where(live_column, routed_rows, 0))
    )
    d_queries = (
        jnp.zeros(queries.shape, jnp.bfloat16)
        .at[local_rows]
        .set(jnp.where(live_column, d_query, 0))
    )
    pair_update = jnp.where(live_column, own_pairs, 0).reshape(capacity, 2, -1)
    key_value_gradient = jnp.zeros(keys_values.shape, jnp.bfloat16).at[local_rows].set(pair_update)
    router_part = jnp.sum(feature_rows.astype(jnp.float32) * d_logit[:, None], axis=0)
    router_grad = sum_over_ctx(router_part)
    return (routed, d_queries, key_value_gradient, router_grad)


def solution(mesh):
    placed = (
        P("ctx", "tp"),
        P("tp"),
        P("ctx", "tp"),
        P("ctx", None, "tp"),
        P("ctx", "tp"),
        P("ctx", None),
        P(),
    )
    return jax.shard_map(
        on_device,
        mesh=mesh,
        in_specs=placed,
        out_specs=(P("ctx", "tp"), P("ctx", "tp"), P("ctx", None, "tp"), P("tp")),
        check_vma=False,
    )
```

```python
import functools
import math

import jax
import jax.numpy as jnp
from jax import lax
from jax.experimental import pallas as pl
from jax.experimental.pallas import tpu as pltpu
from jax.sharding import PartitionSpec as P

HEAD_SIZE = 128
NX, NZ = 4, 8
SLOTS = 64
PAIR = 2 * SLOTS
CHUNK = NZ * SLOTS
SUB = 128
TILE = 16
SCALE = HEAD_SIZE ** -0.5
SCALE2 = SCALE * math.log2(math.e)
MASKED = -1e30
FLOPS_PER_US, BYTES_PER_US = 1153.5e6, 3.69e6
F32, BF16 = jnp.float32, jnp.bfloat16
VMEM = pl.BlockSpec(memory_space=pltpu.VMEM)
SMEM = pl.BlockSpec(memory_space=pltpu.SMEM)
ANY = pl.BlockSpec(memory_space=pl.ANY)


def shard_of(x, z, c):
    return (x * NZ + z) * 2 + c


def move(value, target):
    pairs = []
    for x in range(NX):
        for z in range(NZ):
            for c in range(2):
                place = target(x, z, c)
                if place is not None:
                    pairs.append((shard_of(x, z, c), shard_of(*place)))
    return lax.ppermute(value, "ctx", pairs)


def up_x(k):
    return lambda x, z, c: (x + k, z, c) if x + k < NX else None


def down_x(k):
    return lambda x, z, c: (x - k, z, c) if x >= k else None


def flip_x(bit):
    return lambda x, z, c: (x ^ bit, z, c)


def by_z(k):
    return lambda x, z, c: (x, (z + k) % NZ, c)


def flip_z(x, z, c):
    return (x, z ^ 1, c)


def flip_core(x, z, c):
    return (x, z, c ^ 1)


def flip_tp(value, bit):
    return lax.ppermute(value, "tp", [(i, i ^ bit) for i in range(4)])


def sum_over_tp(value):
    value = value + flip_tp(value, 1)
    return value + flip_tp(value, 2)


def call(kernel, outs, *args, specs=None, scratch=(), after=(), us=0.05):
    skip = len(after)

    def body(*refs):
        kernel(*refs[skip:])

    return pl.pallas_call(
        body,
        out_shape=outs,
        in_specs=[ANY] * skip + list(specs or [VMEM] * len(args)),
        out_specs=jax.tree.map(lambda _: VMEM, outs),
        scratch_shapes=list(scratch),
        compiler_params=pltpu.CompilerParams(vmem_limit_bytes=48 * 1024 * 1024),
        cost_estimate=pl.CostEstimate(
            flops=int(us * FLOPS_PER_US), bytes_accessed=int(us * BYTES_PER_US), transcendentals=0
        ),
    )(*after, *args)


def shape(dims, dtype):
    return jax.ShapeDtypeStruct(dims, dtype)


def dot_tn(a, b):
    return lax.dot_general(a, b, (((0,), (0,)), ((), ())), preferred_element_type=F32)


def dot_nt(a, b):
    return lax.dot_general(a, b, (((1,), (1,)), ((), ())), preferred_element_type=F32)


def dot(a, b):
    return jnp.dot(a, b, preferred_element_type=F32)


def one_hot(chosen_row, tokens, live=None):
    rows = lax.broadcasted_iota(jnp.int32, (tokens, SLOTS), 0)
    hit = rows == chosen_row
    if live is not None:
        hit = hit & (lax.broadcasted_iota(jnp.int32, (tokens, SLOTS), 1) < live)
    return jnp.where(hit, 1.0, 0.0).astype(BF16)


def half_mask(offset):
    i = lax.broadcasted_iota(jnp.int32, (SLOTS, PAIR), 0)
    j = lax.broadcasted_iota(jnp.int32, (SLOTS, PAIR), 1)
    return j == i + offset


def own_column(row, place):
    mine = half_mask((place[0] % 2) * SLOTS)
    return jnp.sum(jnp.where(mine, row, 0.0), axis=1, keepdims=True)


def pair_hot(chosen, tokens, live=SLOTS):
    both = jnp.concatenate([chosen[...], chosen[...]], axis=1)
    lane = lax.broadcasted_iota(jnp.int32, (1, PAIR), 1)
    second = lane >= SLOTS
    target = both * 2 + jnp.where(second, 1, 0)
    slot = lane - jnp.where(second, SLOTS, 0)
    target = jnp.where(slot < live, target, -1)
    rows = lax.broadcasted_iota(jnp.int32, (2 * tokens, PAIR), 0)
    return jnp.where(rows == target, 1.0, 0.0).astype(BF16)


def pick_pairs_kernel(chosen, pairs, rows):
    picked = dot_tn(pair_hot(chosen, pairs.shape[0] // 2), pairs[...]).astype(BF16)
    rows[:, :HEAD_SIZE] = picked[:SLOTS, :]
    rows[:, HEAD_SIZE:] = picked[SLOTS:, :]


def pick_rows_kernel(place, chosen, queries, grads, tokens, weight, qg_rows, t_rows, logit):
    hot = one_hot(chosen[...], queries.shape[0])
    width = queries.shape[1]
    qg_rows[:, :width] = dot_tn(hot, queries[...]).astype(BF16)
    qg_rows[:, width:] = dot_tn(hot, grads[...]).astype(BF16)
    picked = dot_tn(hot, tokens[...]).astype(BF16)
    t_rows[...] = picked
    terms = picked.astype(F32) * weight[...].astype(F32)
    column = jnp.sum(terms, axis=1, keepdims=True)
    mine = half_mask((place[0] % 2) * SLOTS)
    logit[...] = jnp.sum(jnp.where(mine, column, 0.0), axis=0, keepdims=True)


def prepare_kernel(place, own, other, logit, logit_other, qt, qs, gt, logit_sum):
    logit_sum[...] = logit[...] + logit_other[...]
    first = place[0] % 2 == 0
    lanes = qt.shape[1]
    for h in range(own.shape[1] // HEAD_SIZE):
        cols = slice(h * HEAD_SIZE, (h + 1) * HEAD_SIZE)
        mine, theirs = own[:, cols].astype(F32), other[:, cols].astype(F32)
        both = jnp.where(
            first,
            jnp.concatenate([mine, theirs], axis=0),
            jnp.concatenate([theirs, mine], axis=0),
        )
        at = h * PAIR
        if at < lanes:
            qs[at : at + PAIR, :] = both.astype(BF16)
            qt[:, at : at + PAIR] = both.T.astype(BF16)
        else:
            gt[:, at - lanes : at - lanes + PAIR] = both.T.astype(BF16)


def gate_kernel(place, counts, logit, logit_other, gt, gate, dt, ds):
    value = jax.nn.sigmoid(logit[...] + logit_other[...])
    gate[...] = value
    lane = lax.broadcasted_iota(jnp.int32, value.shape, 1)
    chip = place[0] - place[0] % 2
    live = (lane < counts[chip]) | ((lane >= SLOTS) & (lane < SLOTS + counts[chip + 1]))
    live = jnp.broadcast_to(live, (HEAD_SIZE, PAIR))
    for h in range(gt.shape[1] // PAIR):
        cols = slice(h * PAIR, (h + 1) * PAIR)
        scaled = jnp.where(live, gt[:, cols].astype(F32) * value, 0.0)
        dt[:, cols] = scaled.astype(BF16)
        ds[cols, :] = scaled.T.astype(BF16)


def join_sum_kernel(a, b, *refs):
    *refs, total = refs
    total[...] = a[...] + b[...]
    join_kernel(*refs)


def join_kernel(*refs):
    *parts, out = refs
    at = 0
    for part in parts:
        out[at : at + part.shape[0], :] = part[...]
        at += part.shape[0]


def block_plan(place, counts, shift):
    shard = place[0]
    core, chip = shard % 2, shard // 2
    z, x = chip % NZ, chip // NZ
    from_x = (x - shift + NX) % NX
    plan, first = [], jnp.int32(0)
    for j in range(NZ):
        from_z = (((z + (j % 2) * (1 - 2 * (z % 2))) - 2 * (j // 2)) + NZ) % NZ
        from_chip = from_x * NZ + from_z
        live = counts[from_chip * 2 + core]
        ahead = (chip - from_chip) * PAIR - core * SLOTS
        tiles = jnp.where(from_chip <= chip, (live + TILE - 1) // TILE, 0)
        plan.append((live, ahead, tiles, first))
        first = first + tiles
    return plan, first


def pack_rows(plan, pairs, packed, bias):
    packed[...] = jnp.zeros_like(packed)
    bias[...] = jnp.full_like(bias, MASKED)
    slot = lax.broadcasted_iota(jnp.int32, (SLOTS, PAIR), 0)
    lane = lax.broadcasted_iota(jnp.int32, (SLOTS, PAIR), 1)
    for j, (live, ahead, _, first) in enumerate(plan):
        at = pl.ds(pl.multiple_of(first * TILE, TILE), SLOTS)
        packed[at, :] = pairs[j * SLOTS : (j + 1) * SLOTS, :]
        seen = (slot < live) & (slot <= lane + ahead)
        bias[at, :] = jnp.where(seen, 0.0, MASKED)


def scores_of(keys, qt, bias):
    raw = dot(keys, qt[...])
    heads = raw.shape[1] // PAIR
    return raw * SCALE2 + jnp.concatenate([bias] * heads, axis=1)


def forward_kernel(shift, last, place, counts, pairs, qt, *refs):
    if shift == 0:
        acc, stats, packed, bias = refs
        acc[...] = jnp.zeros_like(acc)
        row = lax.broadcasted_iota(jnp.int32, stats.shape, 0)
        stats[...] = jnp.where(row == 0, MASKED, 0.0)
    else:
        if last:
            dt, gt, *refs = refs
        acc_in, stats_in, acc, stats, packed, bias = refs
        acc[...] = acc_in[...]
        stats[...] = stats_in[...]
    plan, tiles = block_plan(place, counts, shift)

    @pl.when(tiles > 0)
    def _():
        pack_rows(plan, pairs, packed, bias)

        def step(i, carry):
            at = pl.ds(pl.multiple_of(i * SUB, SUB), SUB)
            scores = scores_of(packed[at, :HEAD_SIZE], qt, bias[at, :])
            old = stats[0:1, :]
            new = jnp.maximum(old, jnp.max(scores, axis=0, keepdims=True))
            decay = jnp.exp2(old - new)
            weights = jnp.exp2(scores - new)
            stats[0:1, :] = new
            stats[1:2, :] = stats[1:2, :] * decay + jnp.sum(weights, axis=0, keepdims=True)
            mixed = dot_tn(packed[at, HEAD_SIZE:], weights.astype(BF16))
            acc[...] = acc[...] * decay + mixed
            return carry

        lax.fori_loop(0, (tiles * TILE + SUB - 1) // SUB, step, 0)

    if last:
        stats[2:3, :] = jnp.sum(acc[...] * dt[...].astype(F32), axis=0, keepdims=True)
        stats[3:4, :] = jnp.sum(acc[...] * gt[...].astype(F32), axis=0, keepdims=True)


def merge_stats(ours, theirs):
    top = jnp.maximum(ours[0:1, :], theirs[0:1, :])
    a = jnp.exp2(ours[0:1, :] - top)
    b = jnp.exp2(theirs[0:1, :] - top)
    total = ours[1:2, :] * a + theirs[1:2, :] * b
    return top, a, b, total


def backward_kernel(
    shift, place, counts, pairs, qt, qs, dt, ds, ours, theirs, *refs
):
    if shift == 1:
        out, dq, packed, bias, grads = refs
        dq[...] = jnp.zeros_like(dq)
    else:
        if shift == 2:
            part, part_other, *refs = refs
        dq_in, out, dq, *refs = refs
        if shift == 2:
            part_sum, *refs = refs
            part_sum[...] = part[...] + part_other[...]
        packed, bias, grads = refs
        dq[...] = dq_in[...]
    plan, tiles = block_plan(place, counts, shift)
    used = tiles > 0

    @pl.when(used)
    def _():
        pack_rows(plan, pairs, packed, bias)
        top, a, b, total = merge_stats(ours, theirs)
        level = top + jnp.log2(total)
        delta = (ours[2:3, :] * a + theirs[2:3, :] * b) / total

        def step(i, carry):
            at = pl.ds(pl.multiple_of(i * SUB, SUB), SUB)
            keys, values = packed[at, :HEAD_SIZE], packed[at, HEAD_SIZE:]
            probs = jnp.exp2(scores_of(keys, qt, bias[at, :]) - level)
            d_probs = dot(values, dt[...])
            d_scores = (probs * (d_probs - delta)).astype(BF16)
            grads[at, HEAD_SIZE:] = dot(probs.astype(BF16), ds[...])
            grads[at, :HEAD_SIZE] = dot(d_scores, qs[...]) * SCALE
            dq[...] += dot_tn(keys, d_scores)
            return carry

        lax.fori_loop(0, (tiles * TILE + SUB - 1) // SUB, step, 0)
        for j, (_, _, count, first) in enumerate(plan):
            for i in range(SLOTS // TILE):
                at = pl.ds(pl.multiple_of((first + i) * TILE, TILE), TILE)
                piece = jnp.where(i < count, grads[at, :], 0.0)
                out[j * SLOTS + i * TILE : j * SLOTS + (i + 1) * TILE, :] = piece.astype(out.dtype)

    @pl.when(jnp.logical_not(used))
    def _():
        out[...] = jnp.zeros_like(out)


def gate_part_kernel(ours, theirs, part):
    top, a, b, total = merge_stats(ours, theirs)
    dots = (ours[3:4, :] * a + theirs[3:4, :] * b) / total
    part[...] = sum(
        dots[:, h * PAIR : (h + 1) * PAIR] for h in range(dots.shape[1] // PAIR)
    )


def attended_kernel(
    place, counts, chosen, ours, theirs, acc_ours, acc_theirs, gate, dq, routed, dq_own, dq_send
):
    top, a, b, total = merge_stats(ours, theirs)
    a, b = a / total, b / total
    first = place[0] % 2 == 0
    hot = one_hot(chosen[...], routed.shape[0], counts[place[0]])
    factor = own_column(gate[...], place)
    for h in range(acc_ours.shape[1] // PAIR):
        cols = slice(h * PAIR, (h + 1) * PAIR)
        mixed = (acc_ours[:, cols] * a[:, cols] + acc_theirs[:, cols] * b[:, cols]).T
        rows = jnp.where(first, mixed[:SLOTS, :], mixed[SLOTS:, :]).astype(BF16).astype(F32)
        routed[:, cols] = dot(hot, (rows * factor).astype(BF16)).astype(BF16)
        both = dq[:, cols].T
        dq_own[:, cols] = jnp.where(first, both[:SLOTS, :], both[SLOTS:, :])
        dq_send[:, cols] = jnp.where(first, both[SLOTS:, :], both[:SLOTS, :])


def queries_kernel(place, counts, chosen, own, other, out, ready):
    ready[...] = own[0:1, :PAIR]
    hot = one_hot(chosen[...], out.shape[0], counts[place[0]])
    rows = ((own[...] + other[...]) * SCALE).astype(BF16)
    out[...] = dot(hot, rows).astype(BF16)


def add_kernel(a, b, out):
    out[...] = a[...] + b[...]


def router_kernel(place, counts, d_gate, d_gate_other, gate, t_rows, out):
    value = own_column(gate[...], place)
    total = own_column(d_gate[...] + d_gate_other[...], place)
    slot = lax.broadcasted_iota(jnp.int32, (SLOTS, 1), 0)
    d_logit = jnp.where(slot < counts[place[0]], total * value * (1.0 - value), 0.0)
    terms = t_rows[...].astype(F32) * d_logit
    sums = jnp.sum(terms, axis=0, keepdims=True)
    width = out.shape[1]
    out[...] = jnp.zeros_like(out)
    for r in range(sums.shape[1] // width):
        out[r : r + 1, :] = sums[:, r * width : (r + 1) * width]


def put_sum(ref, at, total):
    high = total.astype(BF16)
    ref[at : at + TILE, :] = jnp.concatenate(
        [high.astype(F32), total - high.astype(F32)], axis=0
    ).astype(BF16)


def get_sum(ref, at):
    both = ref[at : at + TILE, :].astype(F32)
    return both[: TILE // 2, :] + both[TILE // 2 :, :]


def sum_x_kernel(own, a, b, c, r0, r1, keep, keep_sum, *sends):
    size = keep.shape[0]
    router = r0[...] + r1[...]
    keep_sum[...] = router
    for i in range(4):
        at = slice(i * size, (i + 1) * size)
        total = own[at, :] + a[at, :].astype(F32) + b[at, :].astype(F32) + c[at, :].astype(F32)
        if i == 0:
            keep[...] = total
        else:
            sends[i - 1][:size, :] = total.astype(BF16)
            put_sum(sends[i - 1], size, router)


def sum_z_kernel(own, own_sum, a, b, c, keep, keep_sum, send):
    size = keep.shape[0]
    full = own.shape[0]
    parts = [ref[:full, :].astype(F32) for ref in (a, b, c)]
    total = own[...] + parts[0] + parts[1] + parts[2]
    router = own_sum[...] + get_sum(a, full) + get_sum(b, full) + get_sum(c, full)
    keep_sum[...] = router
    keep[...] = total[:size, :]
    send[:size, :] = total[size:, :].astype(BF16)
    put_sum(send, size, router)


def last_sum_kernel(own_sum, a, out):
    out[...] = own_sum[...] + get_sum(a, SLOTS)


def pairs_kernel(place, counts, chosen, own, a, out):
    hot = pair_hot(chosen, out.shape[0] // 2, counts[place[0]])
    rows = own[...] + a[:SLOTS, :].astype(F32)
    rows = jnp.concatenate([rows[:, :HEAD_SIZE], rows[:, HEAD_SIZE:]], axis=0).astype(BF16)
    out[...] = dot(hot, rows).astype(BF16)


def on_device(tokens, router_weight, queries, keys_values, routed_grad, chosen, counts):
    place = lax.axis_index("ctx").astype(jnp.int32).reshape(1)
    count = tokens.shape[0]
    width = queries.shape[1]
    lanes = width // HEAD_SIZE * PAIR
    features = tokens.shape[1]
    pair_width = 2 * HEAD_SIZE
    scalars = [SMEM, SMEM]
    packed = [pltpu.VMEM((CHUNK, pair_width), BF16), pltpu.VMEM((CHUNK, PAIR), F32)]

    own_rows = call(
        pick_pairs_kernel,
        shape((SLOTS, pair_width), BF16),
        chosen,
        keys_values.reshape(2 * count, HEAD_SIZE),
        us=0.6,
    )

    pair_row = shape((1, PAIR), F32)
    two = call(
        join_kernel, shape((2 * SLOTS, pair_width), BF16), own_rows, move(own_rows, flip_z)
    )
    neighbours = [move(two, by_z(k)) for k in (2, 4, 6)]
    qg_rows, t_rows, logit = call(
        pick_rows_kernel,
        (shape((SLOTS, 2 * width), BF16), shape((SLOTS, features), BF16), pair_row),
        place,
        chosen,
        queries,
        routed_grad,
        tokens,
        router_weight.reshape(1, features),
        specs=[SMEM] + [VMEM] * 5,
        after=(two,),
        us=0.6,
    )
    turned, stacked = shape((HEAD_SIZE, lanes), BF16), shape((lanes, HEAD_SIZE), BF16)
    qt, qs, gt, logit = call(
        prepare_kernel,
        (turned, stacked, turned, pair_row),
        place,
        qg_rows,
        move(qg_rows, flip_core),
        logit,
        flip_tp(logit, 1),
        specs=[SMEM] + [VMEM] * 4,
        us=0.25,
    )
    chunk, logit = call(
        join_sum_kernel,
        (shape((CHUNK, pair_width), BF16), pair_row),
        logit,
        move(logit, flip_core),
        two,
        *neighbours,
    )
    chunks = [chunk] + [move(chunk, up_x(k)) for k in (1, 2, 3)]

    acc_shape, stats_shape = shape((HEAD_SIZE, lanes), F32), shape((8, lanes), F32)
    state = ()
    for k in range(NX):
        extra = ()
        if k == NX - 1:
            gate, dt, ds = call(
                gate_kernel,
                (pair_row, turned, stacked),
                place,
                counts,
                logit,
                flip_tp(logit, 2),
                gt,
                specs=scalars + [VMEM] * 3,
                after=(state[1],),
                us=0.7,
            )
            extra = (dt, gt)
        state = call(
            functools.partial(forward_kernel, k, k == NX - 1),
            (acc_shape, stats_shape),
            place,
            counts,
            chunks[k],
            qt,
            *extra,
            *state,
            specs=scalars + [VMEM] * (2 + len(extra) + len(state)),
            scratch=packed,
            us=2.2,
        )
    acc, stats = state
    stats_other = move(stats, flip_core)
    acc_other = move(acc, flip_core)

    sums = shape((TILE // 2, pair_width), F32)
    part = call(gate_part_kernel, pair_row, stats, stats_other)

    received, state = {}, ()
    for k in (1, 2, 3, 0):
        extra, more, after = (), (), ()
        if k == 2:
            extra, more = (part, flip_tp(part, 1)), (pair_row,)
        if k == 0:
            router = call(
                router_kernel,
                sums,
                place,
                counts,
                part,
                flip_tp(part, 2),
                gate,
                t_rows,
                specs=scalars + [VMEM] * 4,
                after=(received[1], *state),
                us=0.7,
            )
            after = (router, received[2])
        grad, *state = call(
            functools.partial(backward_kernel, k),
            (shape((CHUNK, pair_width), F32 if k == 0 else BF16), acc_shape, *more),
            place,
            counts,
            chunks[k],
            qt,
            qs,
            dt,
            ds,
            stats,
            stats_other,
            *extra,
            *state,
            specs=scalars + [VMEM] * (7 + len(extra) + len(state)),
            scratch=packed + [pltpu.VMEM((CHUNK, pair_width), F32)],
            after=after,
            us=2.3,
        )
        if k == 2:
            part = state.pop()
        received[k] = grad if k == 0 else move(grad, down_x(k))
    dq = state[0]

    router = call(add_kernel, sums, router, move(router, flip_x(1)), after=(dq,))
    rows = shape((SLOTS, width), F32)
    routed, dq_own, dq_send = call(
        attended_kernel,
        (shape((count, width), BF16), rows, rows),
        place,
        counts,
        chosen,
        stats,
        stats_other,
        acc,
        acc_other,
        gate,
        dq,
        specs=scalars + [VMEM] * 7,
        after=(router,),
        us=1.9,
    )

    half = CHUNK // 4
    keep, keep_sum, *sends = call(
        sum_x_kernel,
        (shape((half, pair_width), F32), sums)
        + (shape((half + TILE, pair_width), BF16),) * 3,
        *[received[k] for k in range(NX)],
        router,
        move(router, flip_x(2)),
        after=(dq_own,),
        us=0.12,
    )
    d_queries, ready = call(
        queries_kernel,
        (shape((count, width), BF16), pair_row),
        place,
        counts,
        chosen,
        dq_own,
        move(dq_send, flip_core),
        specs=scalars + [VMEM] * 3,
        after=(keep,),
        us=1.0,
    )
    keep, keep_sum, send = call(
        sum_z_kernel,
        (
            shape((SLOTS, pair_width), F32),
            sums,
            shape((SLOTS + TILE, pair_width), BF16),
        ),
        keep,
        keep_sum,
        *[move(sends[i], by_z(-k)) for i, k in enumerate((2, 4, 6))],
        after=(ready,),
    )
    got = move(send, flip_z)
    router = call(last_sum_kernel, sums, keep_sum, got)
    router = router + move(router, flip_core)
    pair_grads = call(
        pairs_kernel,
        shape((2 * count, HEAD_SIZE), BF16),
        place,
        counts,
        chosen,
        keep,
        got,
        specs=scalars + [VMEM] * 3,
        us=1.6,
    )
    router_grad = router.reshape(-1)[:features]
    return routed, d_queries, pair_grads.reshape(keys_values.shape), router_grad


def solution(mesh):
    placed = (
        P("ctx", "tp"),
        P("tp"),
        P("ctx", "tp"),
        P("ctx", None, "tp"),
        P("ctx", "tp"),
        P("ctx", None),
        P(),
    )
    return jax.shard_map(
        on_device,
        mesh=mesh,
        in_specs=placed,
        out_specs=(P("ctx", "tp"), P("ctx", "tp"), P("ctx", None, "tp"), P("tp")),
        check_vma=False,
    )
```

```python
import functools
import math

import jax
import jax.numpy as jnp
from jax import lax
from jax.experimental import pallas as pl
from jax.experimental.pallas import tpu as pltpu
from jax.sharding import PartitionSpec as P

HEAD_SIZE = 128
NX, NZ = 4, 8
SLOTS = 64
PAIR = 2 * SLOTS
CHUNK = NZ * SLOTS
GROUP = 256
TILE = 16
SCALE = HEAD_SIZE ** -0.5
SCALE2 = SCALE * math.log2(math.e)
MASKED = -1e30
FLOPS_PER_US, BYTES_PER_US = 1153.5e6, 3.69e6
F32, BF16 = jnp.float32, jnp.bfloat16
VMEM = pl.BlockSpec(memory_space=pltpu.VMEM)
SMEM = pl.BlockSpec(memory_space=pltpu.SMEM)
ANY = pl.BlockSpec(memory_space=pl.ANY)


def shard_of(x, z, c):
    return (x * NZ + z) * 2 + c


def move(value, target):
    pairs = []
    for x in range(NX):
        for z in range(NZ):
            for c in range(2):
                place = target(x, z, c)
                if place is not None:
                    pairs.append((shard_of(x, z, c), shard_of(*place)))
    return lax.ppermute(value, "ctx", pairs)


def up_x(k):
    return lambda x, z, c: (x + k, z, c) if x + k < NX else None


def down_x(k):
    return lambda x, z, c: (x - k, z, c) if x >= k else None


def flip_x(bit):
    return lambda x, z, c: (x ^ bit, z, c)


def by_z(k):
    return lambda x, z, c: (x, (z + k) % NZ, c)


def flip_z(x, z, c):
    return (x, z ^ 1, c)


def flip_core(x, z, c):
    return (x, z, c ^ 1)


def flip_both(x, z, c):
    return (x, z ^ 1, c ^ 1)


def flip_tp(value, bit):
    return lax.ppermute(value, "tp", [(i, i ^ bit) for i in range(4)])


def sum_over_tp(value):
    value = value + flip_tp(value, 1)
    return value + flip_tp(value, 2)


def call(kernel, outs, *args, specs=None, scratch=(), after=(), us=0.05):
    skip = len(after)

    def body(*refs):
        kernel(*refs[skip:])

    return pl.pallas_call(
        body,
        out_shape=outs,
        in_specs=[ANY] * skip + list(specs or [VMEM] * len(args)),
        out_specs=jax.tree.map(lambda _: VMEM, outs),
        scratch_shapes=list(scratch),
        compiler_params=pltpu.CompilerParams(vmem_limit_bytes=48 * 1024 * 1024),
        cost_estimate=pl.CostEstimate(
            flops=int(us * FLOPS_PER_US), bytes_accessed=int(us * BYTES_PER_US), transcendentals=0
        ),
    )(*after, *args)


def shape(dims, dtype):
    return jax.ShapeDtypeStruct(dims, dtype)


def dot_tn(a, b):
    return lax.dot_general(a, b, (((0,), (0,)), ((), ())), preferred_element_type=F32)


def dot_nt(a, b):
    return lax.dot_general(a, b, (((1,), (1,)), ((), ())), preferred_element_type=F32)


def dot(a, b):
    return jnp.dot(a, b, preferred_element_type=F32)


def one_hot(chosen_row, tokens, live=None):
    rows = lax.broadcasted_iota(jnp.int32, (tokens, SLOTS), 0)
    hit = rows == chosen_row
    if live is not None:
        hit = hit & (lax.broadcasted_iota(jnp.int32, (tokens, SLOTS), 1) < live)
    return jnp.where(hit, 1.0, 0.0).astype(BF16)


def half_mask(offset):
    i = lax.broadcasted_iota(jnp.int32, (SLOTS, PAIR), 0)
    j = lax.broadcasted_iota(jnp.int32, (SLOTS, PAIR), 1)
    return j == i + offset


def here():
    shard = lax.axis_index("ctx")
    return shard // (2 * NZ), (shard // 2) % NZ, shard % 2


def own_column(row):
    mine = half_mask(here()[2] * SLOTS)
    return jnp.sum(jnp.where(mine, row, 0.0), axis=1, keepdims=True)


def pair_hot(chosen, tokens, live=SLOTS):
    both = jnp.concatenate([chosen[...], chosen[...]], axis=1)
    lane = lax.broadcasted_iota(jnp.int32, (1, PAIR), 1)
    second = lane >= SLOTS
    target = both * 2 + jnp.where(second, 1, 0)
    slot = lane - jnp.where(second, SLOTS, 0)
    target = jnp.where(slot < live, target, -1)
    rows = lax.broadcasted_iota(jnp.int32, (2 * tokens, PAIR), 0)
    return jnp.where(rows == target, 1.0, 0.0).astype(BF16)


def pick_pairs_kernel(chosen, pairs, rows):
    picked = dot_tn(pair_hot(chosen, pairs.shape[0] // 2), pairs[...]).astype(BF16)
    rows[:, :HEAD_SIZE] = picked[:SLOTS, :]
    rows[:, HEAD_SIZE:] = picked[SLOTS:, :]


def pick_rows_kernel(chosen, queries, grads, tokens, weight, qg_rows, t_rows, logit):
    hot = one_hot(chosen[...], queries.shape[0])
    width = queries.shape[1]
    qg_rows[:, :width] = dot_tn(hot, queries[...]).astype(BF16)
    qg_rows[:, width:] = dot_tn(hot, grads[...]).astype(BF16)
    picked = dot_tn(hot, tokens[...]).astype(BF16)
    t_rows[...] = picked
    terms = picked.astype(F32) * weight[...].astype(F32)
    column = jnp.sum(terms, axis=1, keepdims=True)
    mine = half_mask(here()[2] * SLOTS)
    logit[...] = jnp.sum(jnp.where(mine, column, 0.0), axis=0, keepdims=True)


def prepare_kernel(own, other, logit, logit_other, qt, qs, gt, logit_sum):
    logit_sum[...] = logit[...] + logit_other[...]
    first = here()[2] == 0
    lanes = qt.shape[1]
    for h in range(own.shape[1] // HEAD_SIZE):
        cols = slice(h * HEAD_SIZE, (h + 1) * HEAD_SIZE)
        mine, theirs = own[:, cols].astype(F32), other[:, cols].astype(F32)
        both = jnp.where(
            first,
            jnp.concatenate([mine, theirs], axis=0),
            jnp.concatenate([theirs, mine], axis=0),
        )
        at = h * PAIR
        if at < lanes:
            qs[at : at + PAIR, :] = both.astype(BF16)
            qt[:, at : at + PAIR] = both.T.astype(BF16)
        else:
            gt[:, at - lanes : at - lanes + PAIR] = both.T.astype(BF16)


def gate_kernel(live, logit, logit_other, gt, gate, dt, ds):
    value = jax.nn.sigmoid(logit[...] + logit_other[...])
    gate[...] = value
    kept = jnp.broadcast_to(live[...] > 0.0, (HEAD_SIZE, PAIR))
    for h in range(gt.shape[1] // PAIR):
        cols = slice(h * PAIR, (h + 1) * PAIR)
        scaled = jnp.where(kept, gt[:, cols].astype(F32) * value, 0.0)
        dt[:, cols] = scaled.astype(BF16)
        ds[cols, :] = scaled.T.astype(BF16)


def join_sum_kernel(a, b, *refs):
    *refs, total = refs
    total[...] = a[...] + b[...]
    join_kernel(*refs)


def join_kernel(*refs):
    *parts, out = refs
    at = 0
    for part in parts:
        out[at : at + part.shape[0], :] = part[...]
        at += part.shape[0]


def masks_kernel(counts, chosen, live, hot, both_hot, *biases):
    x, z, core = here()
    chip = x * NZ + z
    lane = lax.broadcasted_iota(jnp.int32, live.shape, 1)
    seen = lane < counts[2 * chip]
    seen = seen | ((lane >= SLOTS) & (lane < SLOTS + counts[2 * chip + 1]))
    live[...] = jnp.where(seen, 1.0, 0.0)
    own = counts[2 * chip + core]
    hot[...] = one_hot(chosen[...], hot.shape[0], own)
    both_hot[...] = pair_hot(chosen, both_hot.shape[0] // 2, own)
    slot = lax.broadcasted_iota(jnp.int32, (SLOTS, PAIR), 0)
    lane = lax.broadcasted_iota(jnp.int32, (SLOTS, PAIR), 1)
    for shift, bias in enumerate(biases):
        from_x = (x - shift + NX) % NX
        for j in range(NZ):
            from_z = (z + (j % 2) * (1 - 2 * (z % 2)) - 2 * (j // 2) + NZ) % NZ
            from_chip = from_x * NZ + from_z
            ahead = (chip - from_chip) * PAIR - core * SLOTS
            seen = (slot < counts[2 * from_chip + core]) & (slot <= lane + ahead)
            bias[j * SLOTS : (j + 1) * SLOTS, :] = jnp.where(seen, 0.0, MASKED)


def lane_groups(ref):
    lanes = ref.shape[1]
    return [slice(a, min(a + GROUP, lanes)) for a in range(0, lanes, GROUP)]


def scores_of(keys, qt, bias):
    raw = dot(keys, qt)
    heads = raw.shape[1] // PAIR
    return raw * SCALE2 + jnp.concatenate([bias] * heads, axis=1)


def forward_kernel(shift, last, bias, pairs, qt, *refs):
    if shift == 0:
        acc, stats = refs
        acc[...] = jnp.zeros_like(acc)
        row = lax.broadcasted_iota(jnp.int32, stats.shape, 0)
        stats[...] = jnp.where(row == 0, MASKED, 0.0)
    else:
        if last:
            dt, gt, *refs = refs
        acc_in, stats_in, acc, stats = refs
        acc[...] = acc_in[...]
        stats[...] = stats_in[...]

    @pl.when(here()[0] >= shift)
    def _():
        keys, values = pairs[:, :HEAD_SIZE], pairs[:, HEAD_SIZE:]
        for cols in lane_groups(qt):
            scores = scores_of(keys, qt[:, cols], bias[...])
            old = stats[0:1, cols]
            new = jnp.maximum(old, jnp.max(scores, axis=0, keepdims=True))
            decay = jnp.exp2(old - new)
            weights = jnp.exp2(scores - new)
            stats[0:1, cols] = new
            total = jnp.sum(weights, axis=0, keepdims=True)
            stats[1:2, cols] = stats[1:2, cols] * decay + total
            acc[:, cols] = acc[:, cols] * decay + dot_tn(values, weights.astype(BF16))

    if last:
        stats[2:3, :] = jnp.sum(acc[...] * dt[...].astype(F32), axis=0, keepdims=True)
        stats[3:4, :] = jnp.sum(acc[...] * gt[...].astype(F32), axis=0, keepdims=True)


def merge_stats(ours, theirs):
    top = jnp.maximum(ours[0:1, :], theirs[0:1, :])
    a = jnp.exp2(ours[0:1, :] - top)
    b = jnp.exp2(theirs[0:1, :] - top)
    total = ours[1:2, :] * a + theirs[1:2, :] * b
    return top, a, b, total


def backward_kernel(shift, bias, pairs, qt, qs, dt, ds, ours, theirs, *refs):
    if shift == 1:
        out, dq = refs
        dq[...] = jnp.zeros_like(dq)
    else:
        if shift == 2:
            part, part_other, *refs = refs
        dq_in, out, dq, *refs = refs
        if shift == 2:
            refs[0][...] = part[...] + part_other[...]
        dq[...] = dq_in[...]
    used = here()[0] >= shift

    @pl.when(used)
    def _():
        top, a, b, total = merge_stats(ours, theirs)
        level = top + jnp.log2(total)
        delta = (ours[2:3, :] * a + theirs[2:3, :] * b) / total
        keys, values = pairs[:, :HEAD_SIZE], pairs[:, HEAD_SIZE:]
        d_values = jnp.zeros(values.shape, F32)
        d_keys = jnp.zeros(keys.shape, F32)
        for cols in lane_groups(qt):
            probs = jnp.exp2(scores_of(keys, qt[:, cols], bias[...]) - level[:, cols])
            d_probs = dot(values, dt[:, cols])
            d_scores = (probs * (d_probs - delta[:, cols])).astype(BF16)
            d_values += dot(probs.astype(BF16), ds[cols, :])
            d_keys += dot(d_scores, qs[cols, :])
            dq[:, cols] += dot_tn(keys, d_scores)
        out[:, :HEAD_SIZE] = (d_keys * SCALE).astype(out.dtype)
        out[:, HEAD_SIZE:] = d_values.astype(out.dtype)

    @pl.when(jnp.logical_not(used))
    def _():
        out[...] = jnp.zeros_like(out)


def gate_part_kernel(ours, theirs, part):
    top, a, b, total = merge_stats(ours, theirs)
    dots = (ours[3:4, :] * a + theirs[3:4, :] * b) / total
    part[...] = sum(
        dots[:, h * PAIR : (h + 1) * PAIR] for h in range(dots.shape[1] // PAIR)
    )


def rows_kernel(
    hot, ours, theirs, acc_ours, acc_theirs, gate, dq_ours, dq_theirs, routed, d_queries, ready
):
    ready[...] = gate[...]
    top, a, b, total = merge_stats(ours, theirs)
    a, b = a / total, b / total
    first = here()[2] == 0
    factor = own_column(gate[...])
    for h in range(acc_ours.shape[1] // PAIR):
        cols = slice(h * PAIR, (h + 1) * PAIR)
        mixed = (acc_ours[:, cols] * a[:, cols] + acc_theirs[:, cols] * b[:, cols]).T
        rows = jnp.where(first, mixed[:SLOTS, :], mixed[SLOTS:, :]).astype(BF16).astype(F32)
        routed[:, cols] = dot(hot[...], (rows * factor).astype(BF16)).astype(BF16)
        both = ((dq_ours[:, cols] + dq_theirs[:, cols]) * SCALE).T
        rows = jnp.where(first, both[:SLOTS, :], both[SLOTS:, :]).astype(BF16)
        d_queries[:, cols] = dot(hot[...], rows).astype(BF16)


def add_kernel(a, b, out):
    out[...] = a[...] + b[...]


def router_kernel(live, d_gate, d_gate_other, gate, t_rows, out):
    value = gate[...]
    d_logit = (d_gate[...] + d_gate_other[...]) * value * (1.0 - value)
    d_logit = own_column(jnp.where(live[...] > 0.0, d_logit, 0.0))
    terms = t_rows[...].astype(F32) * d_logit
    sums = jnp.sum(terms, axis=0, keepdims=True)
    width = out.shape[1]
    out[...] = jnp.zeros_like(out)
    for r in range(sums.shape[1] // width):
        out[r : r + 1, :] = sums[:, r * width : (r + 1) * width]


def put_sum(ref, at, total):
    high = total.astype(BF16)
    ref[at : at + TILE, :] = jnp.concatenate(
        [high.astype(F32), total - high.astype(F32)], axis=0
    ).astype(BF16)


def get_sum(ref, at):
    both = ref[at : at + TILE, :].astype(F32)
    return both[: TILE // 2, :] + both[TILE // 2 :, :]


def sum_x_kernel(own, a, b, c, r0, r1, dq, keep, keep_sum, dq_out, *sends):
    dq_out[...] = dq[...]
    size = keep.shape[0]
    router = r0[...] + r1[...]
    keep_sum[...] = router
    for i in range(4):
        at = slice(i * size, (i + 1) * size)
        total = own[at, :] + a[at, :].astype(F32) + b[at, :].astype(F32) + c[at, :].astype(F32)
        if i == 0:
            keep[...] = total
        else:
            sends[i - 1][:size, :] = total.astype(BF16)
            put_sum(sends[i - 1], size, router)


def sum_z_kernel(own, own_sum, a, b, c, keep, keep_sum, send):
    size = keep.shape[0]
    full = own.shape[0]
    parts = [ref[:full, :].astype(F32) for ref in (a, b, c)]
    total = own[...] + parts[0] + parts[1] + parts[2]
    router = own_sum[...] + get_sum(a, full) + get_sum(b, full) + get_sum(c, full)
    keep_sum[...] = router
    keep[...] = total[:size, :]
    send[:size, :] = total[size:, :].astype(BF16)
    put_sum(send, size, router)


def last_kernel(hot, own, a, r0, r1, r2, out, router):
    rows = own[...] + a[:SLOTS, :].astype(F32)
    rows = jnp.concatenate([rows[:, :HEAD_SIZE], rows[:, HEAD_SIZE:]], axis=0).astype(BF16)
    out[...] = dot(hot[...], rows).astype(BF16)
    total = r0[...] + get_sum(a, SLOTS) + r1[...] + r2[...]
    width = total.shape[1]
    for r in range(router.shape[0] // width):
        router[pl.ds(r * width, width)] = total[r, :]


def on_device(tokens, router_weight, queries, keys_values, routed_grad, chosen, counts):
    count = tokens.shape[0]
    width = queries.shape[1]
    lanes = width // HEAD_SIZE * PAIR
    features = tokens.shape[1]
    pair_width = 2 * HEAD_SIZE

    own_rows = call(
        pick_pairs_kernel,
        shape((SLOTS, pair_width), BF16),
        chosen,
        keys_values.reshape(2 * count, HEAD_SIZE),
        us=0.6,
    )

    pair_row = shape((1, PAIR), F32)
    two = call(
        join_kernel, shape((2 * SLOTS, pair_width), BF16), own_rows, move(own_rows, flip_z)
    )
    live, hot, both_hot, *biases = call(
        masks_kernel,
        (
            pair_row,
            shape((count, SLOTS), BF16),
            shape((2 * count, PAIR), BF16),
            *[shape((CHUNK, PAIR), F32)] * NX,
        ),
        counts,
        chosen,
        specs=[SMEM, VMEM],
        after=(own_rows,),
        us=1.0,
    )
    neighbours = [move(two, by_z(k)) for k in (2, 4, 6)]
    qg_rows, t_rows, logit = call(
        pick_rows_kernel,
        (shape((SLOTS, 2 * width), BF16), shape((SLOTS, features), BF16), pair_row),
        chosen,
        queries,
        routed_grad,
        tokens,
        router_weight.reshape(1, features),
        after=(two, live),
        us=0.6,
    )
    turned, stacked = shape((HEAD_SIZE, lanes), BF16), shape((lanes, HEAD_SIZE), BF16)
    qt, qs, gt, logit = call(
        prepare_kernel,
        (turned, stacked, turned, pair_row),
        qg_rows,
        move(qg_rows, flip_core),
        logit,
        flip_tp(logit, 1),
        us=0.25,
    )
    chunk, logit = call(
        join_sum_kernel,
        (shape((CHUNK, pair_width), BF16), pair_row),
        logit,
        move(logit, flip_core),
        two,
        *neighbours,
    )
    chunks = [chunk] + [move(chunk, up_x(k)) for k in (1, 2, 3)]

    acc_shape, stats_shape = shape((HEAD_SIZE, lanes), F32), shape((8, lanes), F32)
    state = ()
    for k in range(NX):
        extra = ()
        if k == NX - 1:
            gate, dt, ds = call(
                gate_kernel,
                (pair_row, turned, stacked),
                live,
                logit,
                flip_tp(logit, 2),
                gt,
                after=(state[1],),
                us=0.7,
            )
            extra = (dt, gt)
        state = call(
            functools.partial(forward_kernel, k, k == NX - 1),
            (acc_shape, stats_shape),
            biases[k],
            chunks[k],
            qt,
            *extra,
            *state,
            us=2.2,
        )
    acc, stats = state
    stats_other = move(stats, flip_core)
    acc_other = move(acc, flip_core)

    sums = shape((TILE // 2, pair_width), F32)
    part = call(gate_part_kernel, pair_row, stats, stats_other)

    received, state = {}, ()
    for k in (1, 2, 3, 0):
        extra, more, after = (), (), ()
        if k == 2:
            extra, more = (part, flip_tp(part, 1)), (pair_row,)
        if k == 0:
            router = call(
                router_kernel,
                sums,
                live,
                part,
                flip_tp(part, 2),
                gate,
                t_rows,
                after=(received[1], *state),
                us=0.7,
            )
            after = (router, received[2], acc_other)
        grad, *state = call(
            functools.partial(backward_kernel, k),
            (shape((CHUNK, pair_width), F32 if k == 0 else BF16), acc_shape, *more),
            biases[k],
            chunks[k],
            qt,
            qs,
            dt,
            ds,
            stats,
            stats_other,
            *extra,
            *state,
            after=after,
            us=2.3,
        )
        if k == 2:
            part = state.pop()
        received[k] = grad if k == 0 else move(grad, down_x(k))
    dq = state[0]

    router = call(add_kernel, sums, router, move(router, flip_x(1)), after=(dq,))
    half = CHUNK // 4
    keep, keep_sum, dq, *sends = call(
        sum_x_kernel,
        (shape((half, pair_width), F32), sums, acc_shape)
        + (shape((half + TILE, pair_width), BF16),) * 3,
        *[received[k] for k in range(NX)],
        router,
        move(router, flip_x(2)),
        dq,
        us=0.12,
    )
    routed, d_queries, ready = call(
        rows_kernel,
        (shape((count, width), BF16), shape((count, width), BF16), pair_row),
        hot,
        stats,
        stats_other,
        acc,
        acc_other,
        gate,
        dq,
        move(dq, flip_core),
        us=4.0,
    )
    keep, keep_sum, send = call(
        sum_z_kernel,
        (
            shape((SLOTS, pair_width), F32),
            sums,
            shape((SLOTS + TILE, pair_width), BF16),
        ),
        keep,
        keep_sum,
        *[move(sends[i], by_z(-k)) for i, k in enumerate((2, 4, 6))],
        after=(ready,),
    )
    got = move(send, flip_z)
    pair_grads, router_grad = call(
        last_kernel,
        (shape((2 * count, HEAD_SIZE), BF16), shape((features,), F32)),
        both_hot,
        keep,
        got,
        keep_sum,
        move(keep_sum, flip_core),
        move(keep_sum, flip_both),
        us=1.4,
    )
    return routed, d_queries, pair_grads.reshape(keys_values.shape), router_grad


def solution(mesh):
    placed = (
        P("ctx", "tp"),
        P("tp"),
        P("ctx", "tp"),
        P("ctx", None, "tp"),
        P("ctx", "tp"),
        P("ctx", None),
        P(),
    )
    return jax.shard_map(
        on_device,
        mesh=mesh,
        in_specs=placed,
        out_specs=(P("ctx", "tp"), P("ctx", "tp"), P("ctx", None, "tp"), P("tp")),
        check_vma=False,
    )
```

```python
import functools
import math

import jax
import jax.numpy as jnp
from jax import lax
from jax.experimental import pallas as pl
from jax.experimental.pallas import tpu as pltpu
from jax.sharding import PartitionSpec as P

HEAD_SIZE = 128
NX, NZ = 4, 8
SLOTS = 64
PAIR = 2 * SLOTS
CHUNK = NZ * SLOTS
GROUP = 256
TILE = 16
SCALE = HEAD_SIZE ** -0.5
SCALE2 = SCALE * math.log2(math.e)
MASKED = -1e30
FLOPS_PER_US, BYTES_PER_US = 1153.5e6, 3.69e6
F32, BF16 = jnp.float32, jnp.bfloat16
VMEM = pl.BlockSpec(memory_space=pltpu.VMEM)
SMEM = pl.BlockSpec(memory_space=pltpu.SMEM)
ANY = pl.BlockSpec(memory_space=pl.ANY)


def shard_of(x, z, c):
    return (x * NZ + z) * 2 + c


def move(value, target):
    pairs = []
    for x in range(NX):
        for z in range(NZ):
            for c in range(2):
                place = target(x, z, c)
                if place is not None:
                    pairs.append((shard_of(x, z, c), shard_of(*place)))
    return lax.ppermute(value, "ctx", pairs)


def by_x(k):
    return lambda x, z, c: ((x + k) % NX, z, c)


def down_x(least):
    return lambda x, z, c: (x - 1, z, c) if x >= least else None


def last_to_first(x, z, c):
    return (0, z, c) if x == NX - 1 else None


def flip_x(bit):
    return lambda x, z, c: (x ^ bit, z, c)


def by_z(k):
    return lambda x, z, c: (x, (z + k) % NZ, c)


def flip_z(x, z, c):
    return (x, z ^ 1, c)


def flip_core(x, z, c):
    return (x, z, c ^ 1)


def flip_both(x, z, c):
    return (x, z ^ 1, c ^ 1)


def flip_tp(value, bit):
    return lax.ppermute(value, "tp", [(i, i ^ bit) for i in range(4)])


def sum_over_tp(value):
    value = value + flip_tp(value, 1)
    return value + flip_tp(value, 2)


def call(kernel, outs, *args, specs=None, scratch=(), after=(), us=0.05):
    skip = len(after)

    def body(*refs):
        kernel(*refs[skip:])

    return pl.pallas_call(
        body,
        out_shape=outs,
        in_specs=[ANY] * skip + list(specs or [VMEM] * len(args)),
        out_specs=jax.tree.map(lambda _: VMEM, outs),
        scratch_shapes=list(scratch),
        compiler_params=pltpu.CompilerParams(vmem_limit_bytes=48 * 1024 * 1024),
        cost_estimate=pl.CostEstimate(
            flops=int(us * FLOPS_PER_US), bytes_accessed=int(us * BYTES_PER_US), transcendentals=0
        ),
    )(*after, *args)


def shape(dims, dtype):
    return jax.ShapeDtypeStruct(dims, dtype)


def dot_tn(a, b):
    return lax.dot_general(a, b, (((0,), (0,)), ((), ())), preferred_element_type=F32)


def dot_nt(a, b):
    return lax.dot_general(a, b, (((1,), (1,)), ((), ())), preferred_element_type=F32)


def dot(a, b):
    return jnp.dot(a, b, preferred_element_type=F32)


def one_hot(chosen_row, tokens, live=None):
    rows = lax.broadcasted_iota(jnp.int32, (tokens, SLOTS), 0)
    hit = rows == chosen_row
    if live is not None:
        hit = hit & (lax.broadcasted_iota(jnp.int32, (tokens, SLOTS), 1) < live)
    return jnp.where(hit, 1.0, 0.0).astype(BF16)


def half_mask(offset):
    i = lax.broadcasted_iota(jnp.int32, (SLOTS, PAIR), 0)
    j = lax.broadcasted_iota(jnp.int32, (SLOTS, PAIR), 1)
    return j == i + offset


def here():
    shard = lax.axis_index("ctx")
    return shard // (2 * NZ), (shard // 2) % NZ, shard % 2


def own_column(row):
    mine = half_mask(here()[2] * SLOTS)
    return jnp.sum(jnp.where(mine, row, 0.0), axis=1, keepdims=True)


def pair_hot(chosen, tokens, live=SLOTS):
    both = jnp.concatenate([chosen[...], chosen[...]], axis=1)
    lane = lax.broadcasted_iota(jnp.int32, (1, PAIR), 1)
    second = lane >= SLOTS
    target = both * 2 + jnp.where(second, 1, 0)
    slot = lane - jnp.where(second, SLOTS, 0)
    target = jnp.where(slot < live, target, -1)
    rows = lax.broadcasted_iota(jnp.int32, (2 * tokens, PAIR), 0)
    return jnp.where(rows == target, 1.0, 0.0).astype(BF16)


def pick_pairs_kernel(chosen, pairs, rows):
    picked = dot_tn(pair_hot(chosen, pairs.shape[0] // 2), pairs[...]).astype(BF16)
    rows[:, :HEAD_SIZE] = picked[:SLOTS, :]
    rows[:, HEAD_SIZE:] = picked[SLOTS:, :]


def pick_rows_kernel(chosen, queries, grads, tokens, weight, qg_rows, t_rows, logit):
    hot = one_hot(chosen[...], queries.shape[0])
    width = queries.shape[1]
    qg_rows[:, :width] = dot_tn(hot, queries[...]).astype(BF16)
    qg_rows[:, width:] = dot_tn(hot, grads[...]).astype(BF16)
    picked = dot_tn(hot, tokens[...]).astype(BF16)
    t_rows[...] = picked
    terms = picked.astype(F32) * weight[...].astype(F32)
    column = jnp.sum(terms, axis=1, keepdims=True)
    mine = half_mask(here()[2] * SLOTS)
    logit[...] = jnp.sum(jnp.where(mine, column, 0.0), axis=0, keepdims=True)


def prepare_kernel(own, other, qt, qs, gt):
    first = here()[2] == 0
    lanes = qt.shape[1]
    for h in range(own.shape[1] // HEAD_SIZE):
        cols = slice(h * HEAD_SIZE, (h + 1) * HEAD_SIZE)
        mine, theirs = own[:, cols].astype(F32), other[:, cols].astype(F32)
        both = jnp.where(
            first,
            jnp.concatenate([mine, theirs], axis=0),
            jnp.concatenate([theirs, mine], axis=0),
        )
        at = h * PAIR
        if at < lanes:
            qs[at : at + PAIR, :] = both.astype(BF16)
            qt[:, at : at + PAIR] = both.T.astype(BF16)
        else:
            gt[:, at - lanes : at - lanes + PAIR] = both.T.astype(BF16)


def gate_kernel(live, logit, logit_other, gt, gate, dt, ds):
    value = jax.nn.sigmoid(logit[...] + logit_other[...])
    gate[...] = value
    kept = jnp.broadcast_to(live[...] > 0.0, (HEAD_SIZE, PAIR))
    for h in range(gt.shape[1] // PAIR):
        cols = slice(h * PAIR, (h + 1) * PAIR)
        scaled = jnp.where(kept, gt[:, cols].astype(F32) * value, 0.0)
        dt[:, cols] = scaled.astype(BF16)
        ds[cols, :] = scaled.T.astype(BF16)


def join_sum_kernel(a, b, *refs):
    *refs, total = refs
    total[...] = a[...] + b[...]
    join_kernel(*refs)


def join_kernel(*refs):
    *parts, out = refs
    at = 0
    for part in parts:
        out[at : at + part.shape[0], :] = part[...]
        at += part.shape[0]


def masks_kernel(counts, chosen, live, hot, both_hot, *biases):
    x, z, core = here()
    chip = x * NZ + z
    lane = lax.broadcasted_iota(jnp.int32, live.shape, 1)
    seen = lane < counts[2 * chip]
    seen = seen | ((lane >= SLOTS) & (lane < SLOTS + counts[2 * chip + 1]))
    live[...] = jnp.where(seen, 1.0, 0.0)
    own = counts[2 * chip + core]
    hot[...] = one_hot(chosen[...], hot.shape[0], own)
    both_hot[...] = pair_hot(chosen, both_hot.shape[0] // 2, own)
    slot = lax.broadcasted_iota(jnp.int32, (SLOTS, PAIR), 0)
    lane = lax.broadcasted_iota(jnp.int32, (SLOTS, PAIR), 1)
    for shift, bias in enumerate(biases):
        from_x = (x - shift + NX) % NX
        for j in range(NZ):
            from_z = (z + (j % 2) * (1 - 2 * (z % 2)) - 2 * (j // 2) + NZ) % NZ
            from_chip = from_x * NZ + from_z
            ahead = (chip - from_chip) * PAIR - core * SLOTS
            seen = (slot < counts[2 * from_chip + core]) & (slot <= lane + ahead)
            bias[j * SLOTS : (j + 1) * SLOTS, :] = jnp.where(seen, 0.0, MASKED)


def lane_groups(ref):
    lanes = ref.shape[1]
    return [slice(a, min(a + GROUP, lanes)) for a in range(0, lanes, GROUP)]


def scores_of(keys, qt, bias):
    raw = dot(keys, qt)
    heads = raw.shape[1] // PAIR
    return raw * SCALE2 + jnp.concatenate([bias] * heads, axis=1)


def forward_kernel(shift, last, bias, pairs, qt, *refs):
    if shift == 0:
        acc, stats = refs
        acc[...] = jnp.zeros_like(acc)
        row = lax.broadcasted_iota(jnp.int32, stats.shape, 0)
        stats[...] = jnp.where(row == 0, MASKED, 0.0)
    else:
        if last:
            dt, gt, *refs = refs
        acc_in, stats_in, acc, stats = refs
        acc[...] = acc_in[...]
        stats[...] = stats_in[...]

    @pl.when(here()[0] >= shift)
    def _():
        keys, values = pairs[:, :HEAD_SIZE], pairs[:, HEAD_SIZE:]
        for cols in lane_groups(qt):
            scores = scores_of(keys, qt[:, cols], bias[...])
            old = stats[0:1, cols]
            new = jnp.maximum(old, jnp.max(scores, axis=0, keepdims=True))
            decay = jnp.exp2(old - new)
            weights = jnp.exp2(scores - new)
            stats[0:1, cols] = new
            total = jnp.sum(weights, axis=0, keepdims=True)
            stats[1:2, cols] = stats[1:2, cols] * decay + total
            acc[:, cols] = acc[:, cols] * decay + dot_tn(values, weights.astype(BF16))

    if last:
        stats[2:3, :] = jnp.sum(acc[...] * dt[...].astype(F32), axis=0, keepdims=True)
        stats[3:4, :] = jnp.sum(acc[...] * gt[...].astype(F32), axis=0, keepdims=True)


def merge_stats(ours, theirs):
    top = jnp.maximum(ours[0:1, :], theirs[0:1, :])
    a = jnp.exp2(ours[0:1, :] - top)
    b = jnp.exp2(theirs[0:1, :] - top)
    total = ours[1:2, :] * a + theirs[1:2, :] * b
    return top, a, b, total


def backward_kernel(shift, place, bias, pairs, qt, qs, dt, ds, ours, theirs, *refs):
    if place == 0:
        out, dq = refs
        dq[...] = jnp.zeros_like(dq)
    else:
        if place == 1:
            part, part_other, *refs = refs
        dq_in, out, dq, *refs = refs
        if place == 1:
            refs[0][...] = part[...] + part_other[...]
        dq[...] = dq_in[...]
    used = here()[0] >= shift

    @pl.when(used)
    def _():
        top, a, b, total = merge_stats(ours, theirs)
        level = top + jnp.log2(total)
        delta = (ours[2:3, :] * a + theirs[2:3, :] * b) / total
        keys, values = pairs[:, :HEAD_SIZE], pairs[:, HEAD_SIZE:]
        d_values = jnp.zeros(values.shape, F32)
        d_keys = jnp.zeros(keys.shape, F32)
        for cols in lane_groups(qt):
            probs = jnp.exp2(scores_of(keys, qt[:, cols], bias[...]) - level[:, cols])
            d_probs = dot(values, dt[:, cols])
            d_scores = (probs * (d_probs - delta[:, cols])).astype(BF16)
            d_values += dot(probs.astype(BF16), ds[cols, :])
            d_keys += dot(d_scores, qs[cols, :])
            dq[:, cols] += dot_tn(keys, d_scores)
        out[:, :HEAD_SIZE] = (d_keys * SCALE).astype(out.dtype)
        out[:, HEAD_SIZE:] = d_values.astype(out.dtype)

    @pl.when(jnp.logical_not(used))
    def _():
        out[...] = jnp.zeros_like(out)


def gate_part_kernel(ours, theirs, part):
    top, a, b, total = merge_stats(ours, theirs)
    dots = (ours[3:4, :] * a + theirs[3:4, :] * b) / total
    part[...] = sum(
        dots[:, h * PAIR : (h + 1) * PAIR] for h in range(dots.shape[1] // PAIR)
    )


def rows_kernel(
    hot, ours, theirs, acc_ours, acc_theirs, gate, dq_ours, dq_theirs, routed, d_queries, ready
):
    ready[...] = gate[...]
    top, a, b, total = merge_stats(ours, theirs)
    a, b = a / total, b / total
    first = here()[2] == 0
    factor = own_column(gate[...])
    for h in range(acc_ours.shape[1] // PAIR):
        cols = slice(h * PAIR, (h + 1) * PAIR)
        mixed = (acc_ours[:, cols] * a[:, cols] + acc_theirs[:, cols] * b[:, cols]).T
        rows = jnp.where(first, mixed[:SLOTS, :], mixed[SLOTS:, :]).astype(BF16).astype(F32)
        routed[:, cols] = dot(hot[...], (rows * factor).astype(BF16)).astype(BF16)
        both = ((dq_ours[:, cols] + dq_theirs[:, cols]) * SCALE).T
        rows = jnp.where(first, both[:SLOTS, :], both[SLOTS:, :]).astype(BF16)
        d_queries[:, cols] = dot(hot[...], rows).astype(BF16)


def merge_kernel(grads, received, out):
    out[...] = (grads[...] + received[...].astype(F32)).astype(BF16)


def add_kernel(a, b, out):
    out[...] = a[...] + b[...]


def router_kernel(live, d_gate, d_gate_other, gate, t_rows, out):
    value = gate[...]
    d_logit = (d_gate[...] + d_gate_other[...]) * value * (1.0 - value)
    d_logit = own_column(jnp.where(live[...] > 0.0, d_logit, 0.0))
    terms = t_rows[...].astype(F32) * d_logit
    sums = jnp.sum(terms, axis=0, keepdims=True)
    width = out.shape[1]
    out[...] = jnp.zeros_like(out)
    for r in range(sums.shape[1] // width):
        out[r : r + 1, :] = sums[:, r * width : (r + 1) * width]


def put_sum(ref, at, total):
    high = total.astype(BF16)
    ref[at : at + TILE, :] = jnp.concatenate(
        [high.astype(F32), total - high.astype(F32)], axis=0
    ).astype(BF16)


def get_sum(ref, at):
    both = ref[at : at + TILE, :].astype(F32)
    return both[: TILE // 2, :] + both[TILE // 2 :, :]


def sum_x_kernel(own, a, b, r0, r1, dq, keep, keep_sum, dq_out, *sends):
    dq_out[...] = dq[...]
    size = keep.shape[0]
    router = r0[...] + r1[...]
    keep_sum[...] = router
    for i in range(4):
        at = slice(i * size, (i + 1) * size)
        total = own[at, :] + a[at, :].astype(F32) + b[at, :].astype(F32)
        if i == 0:
            keep[...] = total
        else:
            sends[i - 1][:size, :] = total.astype(BF16)
            put_sum(sends[i - 1], size, router)


def sum_z_kernel(own, own_sum, a, b, c, keep, keep_sum, send):
    size = keep.shape[0]
    full = own.shape[0]
    parts = [ref[:full, :].astype(F32) for ref in (a, b, c)]
    total = own[...] + parts[0] + parts[1] + parts[2]
    router = own_sum[...] + get_sum(a, full) + get_sum(b, full) + get_sum(c, full)
    keep_sum[...] = router
    keep[...] = total[:size, :]
    send[:size, :] = total[size:, :].astype(BF16)
    put_sum(send, size, router)


def last_kernel(hot, own, a, r0, r1, r2, out, router):
    rows = own[...] + a[:SLOTS, :].astype(F32)
    rows = jnp.concatenate([rows[:, :HEAD_SIZE], rows[:, HEAD_SIZE:]], axis=0).astype(BF16)
    out[...] = dot(hot[...], rows).astype(BF16)
    total = r0[...] + get_sum(a, SLOTS) + r1[...] + r2[...]
    width = total.shape[1]
    for r in range(router.shape[0] // width):
        router[pl.ds(r * width, width)] = total[r, :]


def on_device(tokens, router_weight, queries, keys_values, routed_grad, chosen, counts):
    count = tokens.shape[0]
    width = queries.shape[1]
    lanes = width // HEAD_SIZE * PAIR
    features = tokens.shape[1]
    pair_width = 2 * HEAD_SIZE

    own_rows = call(
        pick_pairs_kernel,
        shape((SLOTS, pair_width), BF16),
        chosen,
        keys_values.reshape(2 * count, HEAD_SIZE),
        us=0.6,
    )

    pair_row = shape((1, PAIR), F32)
    two = call(
        join_kernel, shape((2 * SLOTS, pair_width), BF16), own_rows, move(own_rows, flip_z)
    )
    live, hot, both_hot, *biases = call(
        masks_kernel,
        (
            pair_row,
            shape((count, SLOTS), BF16),
            shape((2 * count, PAIR), BF16),
            *[shape((CHUNK, PAIR), F32)] * NX,
        ),
        counts,
        chosen,
        specs=[SMEM, VMEM],
        after=(own_rows,),
        us=1.0,
    )
    neighbours = [move(two, by_z(k)) for k in (2, 4, 6)]
    qg_rows, t_rows, logit = call(
        pick_rows_kernel,
        (shape((SLOTS, 2 * width), BF16), shape((SLOTS, features), BF16), pair_row),
        chosen,
        queries,
        routed_grad,
        tokens,
        router_weight.reshape(1, features),
        after=(two, live),
        us=0.6,
    )
    turned, stacked = shape((HEAD_SIZE, lanes), BF16), shape((lanes, HEAD_SIZE), BF16)
    qt, qs, gt = call(
        prepare_kernel,
        (turned, stacked, turned),
        qg_rows,
        move(qg_rows, flip_core),
        us=0.25,
    )
    logit = call(add_kernel, pair_row, logit, flip_tp(logit, 1))
    chunk, logit = call(
        join_sum_kernel,
        (shape((CHUNK, pair_width), BF16), pair_row),
        logit,
        move(logit, flip_core),
        two,
        *neighbours,
    )
    chunks = [chunk] + [move(chunk, by_x(k)) for k in (1, 2, 3)]

    acc_shape, stats_shape = shape((HEAD_SIZE, lanes), F32), shape((8, lanes), F32)
    state = ()
    for k in range(NX):
        extra = ()
        if k == NX - 1:
            gate, dt, ds = call(
                gate_kernel,
                (pair_row, turned, stacked),
                live,
                logit,
                flip_tp(logit, 2),
                gt,
                after=(state[1],),
                us=0.7,
            )
            extra = (dt, gt)
        state = call(
            functools.partial(forward_kernel, k, k == NX - 1),
            (acc_shape, stats_shape),
            biases[k],
            chunks[k],
            qt,
            *extra,
            *state,
            us=2.2,
        )
    acc, stats = state
    stats_other = move(stats, flip_core)
    acc_other = move(acc, flip_core)

    sums = shape((TILE // 2, pair_width), F32)
    part = call(gate_part_kernel, pair_row, stats, stats_other)

    state, order = (), (2, 3, 1, 0)
    for k in order:
        extra, more, after = (), (), ()
        if k == order[1]:
            extra, more = (part, flip_tp(part, 1)), (pair_row,)
        if k == 0:
            after = (router, acc_other, far)
        grad, *state = call(
            functools.partial(backward_kernel, k, order.index(k)),
            (shape((CHUNK, pair_width), F32 if k < 2 else BF16), acc_shape, *more),
            biases[k],
            chunks[k],
            qt,
            qs,
            dt,
            ds,
            stats,
            stats_other,
            *extra,
            *state,
            after=after,
            us=2.3,
        )
        if k == 2:
            handed = move(grad, down_x(2))
        if k == 3:
            part = state.pop()
            far = move(grad, last_to_first)
        if k == 1:
            near = call(merge_kernel, shape((CHUNK, pair_width), BF16), grad, handed, us=0.15)
            router = call(
                router_kernel,
                sums,
                live,
                part,
                flip_tp(part, 2),
                gate,
                t_rows,
                after=(near,),
                us=0.15,
            )
            near = move(near, down_x(1))
            router = call(add_kernel, sums, router, move(router, flip_x(1)))
    dq = state[0]

    half = CHUNK // 4
    keep, keep_sum, dq, *sends = call(
        sum_x_kernel,
        (shape((half, pair_width), F32), sums, acc_shape)
        + (shape((half + TILE, pair_width), BF16),) * 3,
        grad,
        near,
        far,
        router,
        move(router, flip_x(2)),
        dq,
        us=0.12,
    )
    routed, d_queries, ready = call(
        rows_kernel,
        (shape((count, width), BF16), shape((count, width), BF16), pair_row),
        hot,
        stats,
        stats_other,
        acc,
        acc_other,
        gate,
        dq,
        move(dq, flip_core),
        us=4.0,
    )
    keep, keep_sum, send = call(
        sum_z_kernel,
        (
            shape((SLOTS, pair_width), F32),
            sums,
            shape((SLOTS + TILE, pair_width), BF16),
        ),
        keep,
        keep_sum,
        *[move(sends[i], by_z(-k)) for i, k in enumerate((2, 4, 6))],
        after=(ready,),
    )
    got = move(send, flip_z)
    pair_grads, router_grad = call(
        last_kernel,
        (shape((2 * count, HEAD_SIZE), BF16), shape((features,), F32)),
        both_hot,
        keep,
        got,
        keep_sum,
        move(keep_sum, flip_core),
        move(keep_sum, flip_both),
        us=1.4,
    )
    return routed, d_queries, pair_grads.reshape(keys_values.shape), router_grad


def solution(mesh):
    placed = (
        P("ctx", "tp"),
        P("tp"),
        P("ctx", "tp"),
        P("ctx", None, "tp"),
        P("ctx", "tp"),
        P("ctx", None),
        P(),
    )
    return jax.shard_map(
        on_device,
        mesh=mesh,
        in_specs=placed,
        out_specs=(P("ctx", "tp"), P("ctx", "tp"), P("ctx", None, "tp"), P("tp")),
        check_vma=False,
    )
```

```python
import functools
import math

import jax
import jax.numpy as jnp
from jax import lax
from jax.experimental import pallas as pl
from jax.experimental.pallas import tpu as pltpu
from jax.sharding import PartitionSpec as P

HEAD_SIZE = 128
NX, NZ = 4, 8
SLOTS = 64
PAIR = 2 * SLOTS
CHUNK = NZ * SLOTS
GROUP = 256
TILE = 16
SCALE = HEAD_SIZE ** -0.5
SCALE2 = SCALE * math.log2(math.e)
MASKED = -1e30
FLOPS_PER_US, BYTES_PER_US = 1153.5e6, 3.69e6
F32, BF16 = jnp.float32, jnp.bfloat16
VMEM = pl.BlockSpec(memory_space=pltpu.VMEM)
SMEM = pl.BlockSpec(memory_space=pltpu.SMEM)
ANY = pl.BlockSpec(memory_space=pl.ANY)


def shard_of(x, z, c):
    return (x * NZ + z) * 2 + c


def move(value, target):
    pairs = []
    for x in range(NX):
        for z in range(NZ):
            for c in range(2):
                place = target(x, z, c)
                if place is not None:
                    pairs.append((shard_of(x, z, c), shard_of(*place)))
    return lax.ppermute(value, "ctx", pairs)


def by_x(k):
    return lambda x, z, c: ((x + k) % NX, z, c)


def down_x(least):
    return lambda x, z, c: (x - 1, z, c) if x >= least else None


def last_to_first(x, z, c):
    return (0, z, c) if x == NX - 1 else None


def flip_x(bit):
    return lambda x, z, c: (x ^ bit, z, c)


def by_z(k):
    return lambda x, z, c: (x, (z + k) % NZ, c)


def flip_z(x, z, c):
    return (x, z ^ 1, c)


def flip_core(x, z, c):
    return (x, z, c ^ 1)


def flip_both(x, z, c):
    return (x, z ^ 1, c ^ 1)


def flip_tp(value, bit):
    return lax.ppermute(value, "tp", [(i, i ^ bit) for i in range(4)])


def sum_over_tp(value):
    value = value + flip_tp(value, 1)
    return value + flip_tp(value, 2)


def call(kernel, outs, *args, specs=None, scratch=(), after=(), us=0.05):
    skip = len(after)

    def body(*refs):
        kernel(*refs[skip:])

    return pl.pallas_call(
        body,
        out_shape=outs,
        in_specs=[ANY] * skip + list(specs or [VMEM] * len(args)),
        out_specs=jax.tree.map(lambda _: VMEM, outs),
        scratch_shapes=list(scratch),
        compiler_params=pltpu.CompilerParams(vmem_limit_bytes=48 * 1024 * 1024),
        cost_estimate=pl.CostEstimate(
            flops=int(us * FLOPS_PER_US), bytes_accessed=int(us * BYTES_PER_US), transcendentals=0
        ),
    )(*after, *args)


def shape(dims, dtype):
    return jax.ShapeDtypeStruct(dims, dtype)


def dot_tn(a, b):
    return lax.dot_general(a, b, (((0,), (0,)), ((), ())), preferred_element_type=F32)


def dot_nt(a, b):
    return lax.dot_general(a, b, (((1,), (1,)), ((), ())), preferred_element_type=F32)


def dot(a, b):
    return jnp.dot(a, b, preferred_element_type=F32)


def one_hot(chosen_row, tokens, live=None):
    rows = lax.broadcasted_iota(jnp.int32, (tokens, SLOTS), 0)
    hit = rows == chosen_row
    if live is not None:
        hit = hit & (lax.broadcasted_iota(jnp.int32, (tokens, SLOTS), 1) < live)
    return jnp.where(hit, 1.0, 0.0).astype(BF16)


def half_mask(offset):
    i = lax.broadcasted_iota(jnp.int32, (SLOTS, PAIR), 0)
    j = lax.broadcasted_iota(jnp.int32, (SLOTS, PAIR), 1)
    return j == i + offset


def here():
    shard = lax.axis_index("ctx")
    return shard // (2 * NZ), (shard // 2) % NZ, shard % 2


def own_column(row):
    mine = half_mask(here()[2] * SLOTS)
    return jnp.sum(jnp.where(mine, row, 0.0), axis=1, keepdims=True)


def pair_hot(chosen, tokens, live=SLOTS):
    both = jnp.concatenate([chosen[...], chosen[...]], axis=1)
    lane = lax.broadcasted_iota(jnp.int32, (1, PAIR), 1)
    second = lane >= SLOTS
    target = both * 2 + jnp.where(second, 1, 0)
    slot = lane - jnp.where(second, SLOTS, 0)
    target = jnp.where(slot < live, target, -1)
    rows = lax.broadcasted_iota(jnp.int32, (2 * tokens, PAIR), 0)
    return jnp.where(rows == target, 1.0, 0.0).astype(BF16)


def pick_pairs_kernel(chosen, pairs, rows):
    picked = dot_tn(pair_hot(chosen, pairs.shape[0] // 2), pairs[...]).astype(BF16)
    rows[:, :HEAD_SIZE] = picked[:SLOTS, :]
    rows[:, HEAD_SIZE:] = picked[SLOTS:, :]


def pick_rows_kernel(chosen, queries, grads, tokens, weight, qg_rows, t_rows, logit):
    hot = one_hot(chosen[...], queries.shape[0])
    width = queries.shape[1]
    qg_rows[:, :width] = dot_tn(hot, queries[...]).astype(BF16)
    qg_rows[:, width:] = dot_tn(hot, grads[...]).astype(BF16)
    picked = dot_tn(hot, tokens[...]).astype(BF16)
    t_rows[...] = picked
    terms = picked.astype(F32) * weight[...].astype(F32)
    column = jnp.sum(terms, axis=1, keepdims=True)
    mine = half_mask(here()[2] * SLOTS)
    logit[...] = jnp.sum(jnp.where(mine, column, 0.0), axis=0, keepdims=True)


def prepare_kernel(own, other, qt, qs, gt):
    first = here()[2] == 0
    lanes = qt.shape[1]
    for h in range(own.shape[1] // HEAD_SIZE):
        cols = slice(h * HEAD_SIZE, (h + 1) * HEAD_SIZE)
        mine, theirs = own[:, cols].astype(F32), other[:, cols].astype(F32)
        both = jnp.where(
            first,
            jnp.concatenate([mine, theirs], axis=0),
            jnp.concatenate([theirs, mine], axis=0),
        )
        at = h * PAIR
        if at < lanes:
            qs[at : at + PAIR, :] = both.astype(BF16)
            qt[:, at : at + PAIR] = both.T.astype(BF16)
        else:
            gt[:, at - lanes : at - lanes + PAIR] = both.T.astype(BF16)


def gate_kernel(live, logit, logit_other, gt, gate, dt, ds):
    value = jax.nn.sigmoid(logit[...] + logit_other[...])
    gate[...] = value
    kept = jnp.broadcast_to(live[...] > 0.0, (HEAD_SIZE, PAIR))
    for h in range(gt.shape[1] // PAIR):
        cols = slice(h * PAIR, (h + 1) * PAIR)
        scaled = jnp.where(kept, gt[:, cols].astype(F32) * value, 0.0)
        dt[:, cols] = scaled.astype(BF16)
        ds[cols, :] = scaled.T.astype(BF16)


def join_sum_kernel(a, b, *refs):
    *refs, total = refs
    total[...] = a[...] + b[...]
    join_kernel(*refs)


def join_kernel(*refs):
    *parts, out = refs
    at = 0
    for part in parts:
        out[at : at + part.shape[0], :] = part[...]
        at += part.shape[0]


def masks_kernel(counts, chosen, live, hot, both_hot, *biases):
    x, z, core = here()
    chip = x * NZ + z
    lane = lax.broadcasted_iota(jnp.int32, live.shape, 1)
    seen = lane < counts[2 * chip]
    seen = seen | ((lane >= SLOTS) & (lane < SLOTS + counts[2 * chip + 1]))
    live[...] = jnp.where(seen, 1.0, 0.0)
    own = counts[2 * chip + core]
    hot[...] = one_hot(chosen[...], hot.shape[0], own)
    both_hot[...] = pair_hot(chosen, both_hot.shape[0] // 2, own)
    slot = lax.broadcasted_iota(jnp.int32, (SLOTS, PAIR), 0)
    lane = lax.broadcasted_iota(jnp.int32, (SLOTS, PAIR), 1)
    for shift, bias in enumerate(biases):
        from_x = (x - shift + NX) % NX
        for j in range(NZ):
            from_z = (z + (j % 2) * (1 - 2 * (z % 2)) - 2 * (j // 2) + NZ) % NZ
            from_chip = from_x * NZ + from_z
            ahead = (chip - from_chip) * PAIR - core * SLOTS
            seen = (slot < counts[2 * from_chip + core]) & (slot <= lane + ahead)
            bias[j * SLOTS : (j + 1) * SLOTS, :] = jnp.where(seen, 0.0, MASKED)


def lane_groups(ref):
    lanes = ref.shape[1]
    return [slice(a, min(a + GROUP, lanes)) for a in range(0, lanes, GROUP)]


def scores_of(keys, qt, bias):
    raw = dot(keys, qt)
    heads = raw.shape[1] // PAIR
    return raw * SCALE2 + jnp.concatenate([bias] * heads, axis=1)


def forward_kernel(shift, last, bias, pairs, qt, *refs):
    if shift == 0:
        acc, stats = refs
        acc[...] = jnp.zeros_like(acc)
        row = lax.broadcasted_iota(jnp.int32, stats.shape, 0)
        stats[...] = jnp.where(row == 0, MASKED, 0.0)
    else:
        if last:
            dt, gt, *refs = refs
        acc_in, stats_in, acc, stats = refs
        acc[...] = acc_in[...]
        stats[...] = stats_in[...]

    @pl.when(here()[0] >= shift)
    def _():
        keys, values = pairs[:, :HEAD_SIZE], pairs[:, HEAD_SIZE:]
        for cols in lane_groups(qt):
            scores = scores_of(keys, qt[:, cols], bias[...])
            old = stats[0:1, cols]
            new = jnp.maximum(old, jnp.max(scores, axis=0, keepdims=True))
            decay = jnp.exp2(old - new)
            weights = jnp.exp2(scores - new)
            stats[0:1, cols] = new
            total = jnp.sum(weights, axis=0, keepdims=True)
            stats[1:2, cols] = stats[1:2, cols] * decay + total
            acc[:, cols] = acc[:, cols] * decay + dot_tn(values, weights.astype(BF16))

    if last:
        stats[2:3, :] = jnp.sum(acc[...] * dt[...].astype(F32), axis=0, keepdims=True)
        stats[3:4, :] = jnp.sum(acc[...] * gt[...].astype(F32), axis=0, keepdims=True)


def merge_stats(ours, theirs):
    top = jnp.maximum(ours[0:1, :], theirs[0:1, :])
    a = jnp.exp2(ours[0:1, :] - top)
    b = jnp.exp2(theirs[0:1, :] - top)
    total = ours[1:2, :] * a + theirs[1:2, :] * b
    return top, a, b, total


def backward_kernel(shift, place, bias, pairs, qt, qs, dt, ds, ours, theirs, *refs):
    if place == 0:
        out, dq = refs
        dq[...] = jnp.zeros_like(dq)
    else:
        if place == 1:
            part, part_other, *refs = refs
        dq_in, out, dq, *refs = refs
        if place == 1:
            refs[0][...] = part[...] + part_other[...]
        dq[...] = dq_in[...]
    used = here()[0] >= shift

    @pl.when(used)
    def _():
        top, a, b, total = merge_stats(ours, theirs)
        level = top + jnp.log2(total)
        delta = (ours[2:3, :] * a + theirs[2:3, :] * b) / total
        keys, values = pairs[:, :HEAD_SIZE], pairs[:, HEAD_SIZE:]
        d_values = jnp.zeros(values.shape, F32)
        d_keys = jnp.zeros(keys.shape, F32)
        for cols in lane_groups(qt):
            probs = jnp.exp2(scores_of(keys, qt[:, cols], bias[...]) - level[:, cols])
            d_probs = dot(values, dt[:, cols])
            d_scores = (probs * (d_probs - delta[:, cols])).astype(BF16)
            d_values += dot(probs.astype(BF16), ds[cols, :])
            d_keys += dot(d_scores, qs[cols, :])
            dq[:, cols] += dot_tn(keys, d_scores)
        out[:, :HEAD_SIZE] = (d_keys * SCALE).astype(out.dtype)
        out[:, HEAD_SIZE:] = d_values.astype(out.dtype)

    @pl.when(jnp.logical_not(used))
    def _():
        out[...] = jnp.zeros_like(out)


def gate_part_kernel(ours, theirs, part):
    top, a, b, total = merge_stats(ours, theirs)
    dots = (ours[3:4, :] * a + theirs[3:4, :] * b) / total
    part[...] = sum(
        dots[:, h * PAIR : (h + 1) * PAIR] for h in range(dots.shape[1] // PAIR)
    )


def rows_kernel(
    hot, ours, theirs, acc_ours, acc_theirs, gate, dq_ours, dq_theirs, routed, d_queries, ready
):
    ready[...] = gate[...]
    top, a, b, total = merge_stats(ours, theirs)
    a, b = a / total, b / total
    first = here()[2] == 0
    factor = own_column(gate[...])
    for h in range(acc_ours.shape[1] // PAIR):
        cols = slice(h * PAIR, (h + 1) * PAIR)
        mixed = (acc_ours[:, cols] * a[:, cols] + acc_theirs[:, cols] * b[:, cols]).T
        rows = jnp.where(first, mixed[:SLOTS, :], mixed[SLOTS:, :]).astype(BF16).astype(F32)
        routed[:, cols] = dot(hot[...], (rows * factor).astype(BF16)).astype(BF16)
        both = ((dq_ours[:, cols] + dq_theirs[:, cols]) * SCALE).T
        rows = jnp.where(first, both[:SLOTS, :], both[SLOTS:, :]).astype(BF16)
        d_queries[:, cols] = dot(hot[...], rows).astype(BF16)


def merge_kernel(grads, received, out):
    out[...] = (grads[...] + received[...].astype(F32)).astype(BF16)


def add_kernel(a, b, out):
    out[...] = a[...] + b[...]


def router_kernel(live, d_gate, d_gate_other, gate, t_rows, out):
    value = gate[...]
    d_logit = (d_gate[...] + d_gate_other[...]) * value * (1.0 - value)
    d_logit = own_column(jnp.where(live[...] > 0.0, d_logit, 0.0))
    terms = t_rows[...].astype(F32) * d_logit
    sums = jnp.sum(terms, axis=0, keepdims=True)
    width = out.shape[1]
    out[...] = jnp.zeros_like(out)
    for r in range(sums.shape[1] // width):
        out[r : r + 1, :] = sums[:, r * width : (r + 1) * width]


def put_sum(ref, at, total):
    high = total.astype(BF16)
    ref[at : at + TILE, :] = jnp.concatenate(
        [high.astype(F32), total - high.astype(F32)], axis=0
    ).astype(BF16)


def get_sum(ref, at):
    both = ref[at : at + TILE, :].astype(F32)
    return both[: TILE // 2, :] + both[TILE // 2 :, :]


def sum_x_kernel(own, a, b, r0, r1, keep, router, send):
    size = keep.shape[0]
    router[...] = r0[...] + r1[...]
    for i in range(CHUNK // SLOTS):
        at = slice(i * SLOTS, (i + 1) * SLOTS)
        to = slice(i // 2 * SLOTS, (i // 2 + 1) * SLOTS)
        total = own[at, :] + a[at, :].astype(F32) + b[at, :].astype(F32)
        if i % 2 == 0:
            keep[to, :] = total
        else:
            send[to, :] = total.astype(BF16)
    put_sum(send, size, router[...])


def sum_z_kernel(own, a, r0, r1, r2, dq, keep, router, dq_out, *sends):
    dq_out[...] = dq[...]
    size = keep.shape[0]
    full = own.shape[0]
    total = own[...] + a[:full, :].astype(F32)
    router[...] = r0[...] + get_sum(a, full) + r1[...] + r2[...]
    keep[...] = total[:size, :]
    for i, send in enumerate(sends, 1):
        send[:size, :] = total[i * size : (i + 1) * size, :].astype(BF16)
        put_sum(send, size, router[...])


def last_kernel(hot, own, r0, a, b, c, out, router):
    rows, total = own[...], r0[...]
    for part in (a, b, c):
        rows = rows + part[:SLOTS, :].astype(F32)
        total = total + get_sum(part, SLOTS)
    rows = jnp.concatenate([rows[:, :HEAD_SIZE], rows[:, HEAD_SIZE:]], axis=0).astype(BF16)
    out[...] = dot(hot[...], rows).astype(BF16)
    width = total.shape[1]
    for r in range(router.shape[0] // width):
        router[pl.ds(r * width, width)] = total[r, :]


def on_device(tokens, router_weight, queries, keys_values, routed_grad, chosen, counts):
    count = tokens.shape[0]
    width = queries.shape[1]
    lanes = width // HEAD_SIZE * PAIR
    features = tokens.shape[1]
    pair_width = 2 * HEAD_SIZE

    own_rows = call(
        pick_pairs_kernel,
        shape((SLOTS, pair_width), BF16),
        chosen,
        keys_values.reshape(2 * count, HEAD_SIZE),
        us=0.6,
    )

    pair_row = shape((1, PAIR), F32)
    two = call(
        join_kernel, shape((2 * SLOTS, pair_width), BF16), own_rows, move(own_rows, flip_z)
    )
    live, hot, both_hot, *biases = call(
        masks_kernel,
        (
            pair_row,
            shape((count, SLOTS), BF16),
            shape((2 * count, PAIR), BF16),
            *[shape((CHUNK, PAIR), F32)] * NX,
        ),
        counts,
        chosen,
        specs=[SMEM, VMEM],
        after=(own_rows,),
        us=1.0,
    )
    neighbours = [move(two, by_z(k)) for k in (2, 4, 6)]
    qg_rows, t_rows, logit = call(
        pick_rows_kernel,
        (shape((SLOTS, 2 * width), BF16), shape((SLOTS, features), BF16), pair_row),
        chosen,
        queries,
        routed_grad,
        tokens,
        router_weight.reshape(1, features),
        after=(two, live),
        us=0.6,
    )
    turned, stacked = shape((HEAD_SIZE, lanes), BF16), shape((lanes, HEAD_SIZE), BF16)
    qt, qs, gt = call(
        prepare_kernel,
        (turned, stacked, turned),
        qg_rows,
        move(qg_rows, flip_core),
        us=0.25,
    )
    logit = call(add_kernel, pair_row, logit, flip_tp(logit, 1))
    chunk, logit = call(
        join_sum_kernel,
        (shape((CHUNK, pair_width), BF16), pair_row),
        logit,
        move(logit, flip_core),
        two,
        *neighbours,
    )
    chunks = [chunk] + [move(chunk, by_x(k)) for k in (1, 2, 3)]

    acc_shape, stats_shape = shape((HEAD_SIZE, lanes), F32), shape((8, lanes), F32)
    state = ()
    for k in range(NX):
        extra = ()
        if k == NX - 1:
            gate, dt, ds = call(
                gate_kernel,
                (pair_row, turned, stacked),
                live,
                logit,
                flip_tp(logit, 2),
                gt,
                after=(state[1],),
                us=0.7,
            )
            extra = (dt, gt)
        state = call(
            functools.partial(forward_kernel, k, k == NX - 1),
            (acc_shape, stats_shape),
            biases[k],
            chunks[k],
            qt,
            *extra,
            *state,
            us=0.3,
        )
    acc, stats = state
    stats_other = move(stats, flip_core)
    acc_other = move(acc, flip_core)

    sums = shape((TILE // 2, pair_width), F32)
    part = call(gate_part_kernel, pair_row, stats, stats_other)

    state, order = (), (2, 3, 1, 0)
    for k in order:
        extra, more, after = (), (), ()
        if k == order[1]:
            extra, more = (part, flip_tp(part, 1)), (pair_row,)
        if k == 0:
            after = (router, acc_other, far)
        grad, *state = call(
            functools.partial(backward_kernel, k, order.index(k)),
            (shape((CHUNK, pair_width), F32 if k < 2 else BF16), acc_shape, *more),
            biases[k],
            chunks[k],
            qt,
            qs,
            dt,
            ds,
            stats,
            stats_other,
            *extra,
            *state,
            after=after,
            us=2.3,
        )
        if k == 2:
            handed = move(grad, down_x(2))
        if k == 3:
            part = state.pop()
            far = move(grad, last_to_first)
        if k == 1:
            near = call(merge_kernel, shape((CHUNK, pair_width), BF16), grad, handed, us=0.15)
            router = call(
                router_kernel,
                sums,
                live,
                part,
                flip_tp(part, 2),
                gate,
                t_rows,
                after=(near,),
                us=0.15,
            )
            near = move(near, down_x(1))
            router = call(add_kernel, sums, router, move(router, flip_x(1)))
    dq = state[0]

    half = CHUNK // 2
    keep, router, send = call(
        sum_x_kernel,
        (
            shape((half, pair_width), F32),
            sums,
            shape((half + TILE, pair_width), BF16),
        ),
        grad,
        near,
        far,
        router,
        move(router, flip_x(2)),
        us=0.12,
    )
    keep, router, dq, *sends = call(
        sum_z_kernel,
        (shape((SLOTS, pair_width), F32), sums, acc_shape)
        + (shape((SLOTS + TILE, pair_width), BF16),) * 3,
        keep,
        move(send, flip_z),
        router,
        move(router, flip_core),
        move(router, flip_both),
        dq,
    )
    routed, d_queries, ready = call(
        rows_kernel,
        (shape((count, width), BF16), shape((count, width), BF16), pair_row),
        hot,
        stats,
        stats_other,
        acc,
        acc_other,
        gate,
        dq,
        move(dq, flip_core),
        us=0.1,
    )
    pair_grads, router_grad = call(
        last_kernel,
        (shape((2 * count, HEAD_SIZE), BF16), shape((features,), F32)),
        both_hot,
        keep,
        router,
        *[move(sends[i], by_z(-k)) for i, k in enumerate((2, 4, 6))],
        after=(ready,),
        us=1.4,
    )
    return routed, d_queries, pair_grads.reshape(keys_values.shape), router_grad


def solution(mesh):
    placed = (
        P("ctx", "tp"),
        P("tp"),
        P("ctx", "tp"),
        P("ctx", None, "tp"),
        P("ctx", "tp"),
        P("ctx", None),
        P(),
    )
    return jax.shard_map(
        on_device,
        mesh=mesh,
        in_specs=placed,
        out_specs=(P("ctx", "tp"), P("ctx", "tp"), P("ctx", None, "tp"), P("tp")),
        check_vma=False,
    )
```

```python
import functools
import math

import jax
import jax.numpy as jnp
from jax import lax
from jax.experimental import pallas as pl
from jax.experimental.pallas import tpu as pltpu
from jax.sharding import PartitionSpec as P

HEAD_SIZE = 128
NX, NZ = 4, 8
SLOTS = 64
PAIR = 2 * SLOTS
CHUNK = NZ * SLOTS
GROUP = 256
TILE = 16
SCALE = HEAD_SIZE ** -0.5
SCALE2 = SCALE * math.log2(math.e)
MASKED = -1e30
FLOPS_PER_US, BYTES_PER_US = 1153.5e6, 3.69e6
F32, BF16 = jnp.float32, jnp.bfloat16
VMEM = pl.BlockSpec(memory_space=pltpu.VMEM)
SMEM = pl.BlockSpec(memory_space=pltpu.SMEM)
ANY = pl.BlockSpec(memory_space=pl.ANY)


def shard_of(x, z, c):
    return (x * NZ + z) * 2 + c


def move(value, target):
    pairs = []
    for x in range(NX):
        for z in range(NZ):
            for c in range(2):
                place = target(x, z, c)
                if place is not None:
                    pairs.append((shard_of(x, z, c), shard_of(*place)))
    return lax.ppermute(value, "ctx", pairs)


def by_x(k):
    return lambda x, z, c: ((x + k) % NX, z, c)


def down_x(least):
    return lambda x, z, c: (x - 1, z, c) if x >= least else None


def last_to_first(x, z, c):
    return (0, z, c) if x == NX - 1 else None


def flip_x(bit):
    return lambda x, z, c: (x ^ bit, z, c)


def by_z(k):
    return lambda x, z, c: (x, (z + k) % NZ, c)


def flip_z(x, z, c):
    return (x, z ^ 1, c)


def flip_core(x, z, c):
    return (x, z, c ^ 1)


def flip_both(x, z, c):
    return (x, z ^ 1, c ^ 1)


def flip_tp(value, bit):
    return lax.ppermute(value, "tp", [(i, i ^ bit) for i in range(4)])


def sum_over_tp(value):
    value = value + flip_tp(value, 1)
    return value + flip_tp(value, 2)


def call(kernel, outs, *args, specs=None, scratch=(), after=(), us=0.05):
    skip = len(after)

    def body(*refs):
        kernel(*refs[skip:])

    return pl.pallas_call(
        body,
        out_shape=outs,
        in_specs=[ANY] * skip + list(specs or [VMEM] * len(args)),
        out_specs=jax.tree.map(lambda _: VMEM, outs),
        scratch_shapes=list(scratch),
        compiler_params=pltpu.CompilerParams(vmem_limit_bytes=48 * 1024 * 1024),
        cost_estimate=pl.CostEstimate(
            flops=int(us * FLOPS_PER_US), bytes_accessed=int(us * BYTES_PER_US), transcendentals=0
        ),
    )(*after, *args)


def shape(dims, dtype):
    return jax.ShapeDtypeStruct(dims, dtype)


def dot_tn(a, b):
    return lax.dot_general(a, b, (((0,), (0,)), ((), ())), preferred_element_type=F32)


def dot_nt(a, b):
    return lax.dot_general(a, b, (((1,), (1,)), ((), ())), preferred_element_type=F32)


def dot(a, b):
    return jnp.dot(a, b, preferred_element_type=F32)


def one_hot(chosen_row, tokens, live=None):
    rows = lax.broadcasted_iota(jnp.int32, (tokens, SLOTS), 0)
    hit = rows == chosen_row
    if live is not None:
        hit = hit & (lax.broadcasted_iota(jnp.int32, (tokens, SLOTS), 1) < live)
    return jnp.where(hit, 1.0, 0.0).astype(BF16)


def half_mask(offset):
    i = lax.broadcasted_iota(jnp.int32, (SLOTS, PAIR), 0)
    j = lax.broadcasted_iota(jnp.int32, (SLOTS, PAIR), 1)
    return j == i + offset


def here():
    shard = lax.axis_index("ctx")
    return shard // (2 * NZ), (shard // 2) % NZ, shard % 2


def own_column(row):
    mine = half_mask(here()[2] * SLOTS)
    return jnp.sum(jnp.where(mine, row, 0.0), axis=1, keepdims=True)


def pair_hot(chosen, tokens, live=SLOTS):
    both = jnp.concatenate([chosen[...], chosen[...]], axis=1)
    lane = lax.broadcasted_iota(jnp.int32, (1, PAIR), 1)
    second = lane >= SLOTS
    target = both * 2 + jnp.where(second, 1, 0)
    slot = lane - jnp.where(second, SLOTS, 0)
    target = jnp.where(slot < live, target, -1)
    rows = lax.broadcasted_iota(jnp.int32, (2 * tokens, PAIR), 0)
    return jnp.where(rows == target, 1.0, 0.0).astype(BF16)


def pick_pairs_kernel(chosen, pairs, rows):
    picked = dot_tn(pair_hot(chosen, pairs.shape[0] // 2), pairs[...]).astype(BF16)
    rows[:, :HEAD_SIZE] = picked[:SLOTS, :]
    rows[:, HEAD_SIZE:] = picked[SLOTS:, :]


def pick_rows_kernel(chosen, queries, grads, tokens, weight, qg_rows, t_rows, logit):
    hot = one_hot(chosen[...], queries.shape[0])
    width = queries.shape[1]
    qg_rows[:, :width] = dot_tn(hot, queries[...]).astype(BF16)
    qg_rows[:, width:] = dot_tn(hot, grads[...]).astype(BF16)
    picked = dot_tn(hot, tokens[...]).astype(BF16)
    t_rows[...] = picked
    terms = picked.astype(F32) * weight[...].astype(F32)
    column = jnp.sum(terms, axis=1, keepdims=True)
    mine = half_mask(here()[2] * SLOTS)
    logit[...] = jnp.sum(jnp.where(mine, column, 0.0), axis=0, keepdims=True)


def prepare_kernel(own, other, qt, qs, gt):
    first = here()[2] == 0
    lanes = qt.shape[1]
    for h in range(own.shape[1] // HEAD_SIZE):
        cols = slice(h * HEAD_SIZE, (h + 1) * HEAD_SIZE)
        mine, theirs = own[:, cols].astype(F32), other[:, cols].astype(F32)
        both = jnp.where(
            first,
            jnp.concatenate([mine, theirs], axis=0),
            jnp.concatenate([theirs, mine], axis=0),
        )
        at = h * PAIR
        if at < lanes:
            qs[at : at + PAIR, :] = both.astype(BF16)
            qt[:, at : at + PAIR] = both.T.astype(BF16)
        else:
            gt[:, at - lanes : at - lanes + PAIR] = both.T.astype(BF16)


def gate_kernel(live, logit, logit_other, gt, gate, dt, ds):
    value = jax.nn.sigmoid(logit[...] + logit_other[...])
    gate[...] = value
    kept = jnp.broadcast_to(live[...] > 0.0, (HEAD_SIZE, PAIR))
    for h in range(gt.shape[1] // PAIR):
        cols = slice(h * PAIR, (h + 1) * PAIR)
        scaled = jnp.where(kept, gt[:, cols].astype(F32) * value, 0.0)
        dt[:, cols] = scaled.astype(BF16)
        ds[cols, :] = scaled.T.astype(BF16)


def join_sum_kernel(a, b, *refs):
    *refs, total = refs
    total[...] = a[...] + b[...]
    join_kernel(*refs)


def join_kernel(*refs):
    *parts, out = refs
    at = 0
    for part in parts:
        out[at : at + part.shape[0], :] = part[...]
        at += part.shape[0]


def masks_kernel(counts, chosen, live, hot, both_hot, *biases):
    x, z, core = here()
    chip = x * NZ + z
    lane = lax.broadcasted_iota(jnp.int32, live.shape, 1)
    seen = lane < counts[2 * chip]
    seen = seen | ((lane >= SLOTS) & (lane < SLOTS + counts[2 * chip + 1]))
    live[...] = jnp.where(seen, 1.0, 0.0)
    own = counts[2 * chip + core]
    hot[...] = one_hot(chosen[...], hot.shape[0], own)
    both_hot[...] = pair_hot(chosen, both_hot.shape[0] // 2, own)
    slot = lax.broadcasted_iota(jnp.int32, (SLOTS, PAIR), 0)
    lane = lax.broadcasted_iota(jnp.int32, (SLOTS, PAIR), 1)
    for shift, bias in enumerate(biases):
        from_x = (x - shift + NX) % NX
        for j in range(NZ):
            from_z = (z + (j % 2) * (1 - 2 * (z % 2)) - 2 * (j // 2) + NZ) % NZ
            from_chip = from_x * NZ + from_z
            ahead = (chip - from_chip) * PAIR - core * SLOTS
            seen = (slot < counts[2 * from_chip + core]) & (slot <= lane + ahead)
            bias[j * SLOTS : (j + 1) * SLOTS, :] = jnp.where(seen, 0.0, MASKED)


def lane_groups(ref, size=GROUP):
    lanes = ref.shape[1]
    return [slice(a, min(a + size, lanes)) for a in range(0, lanes, size)]


def scores_of(keys, qt, bias):
    raw = dot(keys, qt)
    heads = raw.shape[1] // PAIR
    return raw * SCALE2 + jnp.concatenate([bias] * heads, axis=1)


def forward_kernel(shift, last, bias, pairs, qt, *refs):
    if shift == 0:
        acc, stats = refs
        acc[...] = jnp.zeros_like(acc)
        row = lax.broadcasted_iota(jnp.int32, stats.shape, 0)
        stats[...] = jnp.where(row == 0, MASKED, 0.0)
    else:
        if last:
            dt, gt, *refs = refs
        acc_in, stats_in, acc, stats = refs
        acc[...] = acc_in[...]
        stats[...] = stats_in[...]

    @pl.when(here()[0] >= shift)
    def _():
        keys, values = pairs[:, :HEAD_SIZE], pairs[:, HEAD_SIZE:]
        for cols in lane_groups(qt, PAIR):
            scores = scores_of(keys, qt[:, cols], bias[...])
            old = stats[0:1, cols]
            new = jnp.maximum(old, jnp.max(scores, axis=0, keepdims=True))
            decay = jnp.exp2(old - new)
            weights = jnp.exp2(scores - new)
            stats[0:1, cols] = new
            total = jnp.sum(weights, axis=0, keepdims=True)
            stats[1:2, cols] = stats[1:2, cols] * decay + total
            acc[:, cols] = acc[:, cols] * decay + dot_tn(values, weights.astype(BF16))

    if last:
        stats[2:3, :] = jnp.sum(acc[...] * dt[...].astype(F32), axis=0, keepdims=True)
        stats[3:4, :] = jnp.sum(acc[...] * gt[...].astype(F32), axis=0, keepdims=True)


def merge_stats(ours, theirs):
    top = jnp.maximum(ours[0:1, :], theirs[0:1, :])
    a = jnp.exp2(ours[0:1, :] - top)
    b = jnp.exp2(theirs[0:1, :] - top)
    total = ours[1:2, :] * a + theirs[1:2, :] * b
    return top, a, b, total


def backward_kernel(shift, place, bias, pairs, qt, qs, dt, ds, ours, theirs, *refs):
    if place == 0:
        out, dq = refs
        dq[...] = jnp.zeros_like(dq)
    else:
        if place == 1:
            part, part_other, *refs = refs
        dq_in, out, dq, *refs = refs
        if place == 1:
            refs[0][...] = part[...] + part_other[...]
        dq[...] = dq_in[...]
    used = here()[0] >= shift

    @pl.when(used)
    def _():
        top, a, b, total = merge_stats(ours, theirs)
        level = top + jnp.log2(total)
        delta = (ours[2:3, :] * a + theirs[2:3, :] * b) / total
        keys, values = pairs[:, :HEAD_SIZE], pairs[:, HEAD_SIZE:]
        d_values = jnp.zeros(values.shape, F32)
        d_keys = jnp.zeros(keys.shape, F32)
        for cols in lane_groups(qt):
            probs = jnp.exp2(scores_of(keys, qt[:, cols], bias[...]) - level[:, cols])
            d_probs = dot(values, dt[:, cols])
            d_scores = (probs * (d_probs - delta[:, cols])).astype(BF16)
            d_values += dot(probs.astype(BF16), ds[cols, :])
            d_keys += dot(d_scores, qs[cols, :])
            dq[:, cols] += dot_tn(keys, d_scores)
        out[:, :HEAD_SIZE] = (d_keys * SCALE).astype(out.dtype)
        out[:, HEAD_SIZE:] = d_values.astype(out.dtype)

    @pl.when(jnp.logical_not(used))
    def _():
        out[...] = jnp.zeros_like(out)


def gate_part_kernel(ours, theirs, part):
    top, a, b, total = merge_stats(ours, theirs)
    dots = (ours[3:4, :] * a + theirs[3:4, :] * b) / total
    part[...] = sum(
        dots[:, h * PAIR : (h + 1) * PAIR] for h in range(dots.shape[1] // PAIR)
    )


def rows_kernel(
    hot, ours, theirs, acc_ours, acc_theirs, gate, dq_ours, dq_theirs, routed, d_queries, ready
):
    ready[...] = gate[...]
    top, a, b, total = merge_stats(ours, theirs)
    a, b = a / total, b / total
    first = here()[2] == 0
    factor = own_column(gate[...])
    for h in range(acc_ours.shape[1] // PAIR):
        cols = slice(h * PAIR, (h + 1) * PAIR)
        mixed = (acc_ours[:, cols] * a[:, cols] + acc_theirs[:, cols] * b[:, cols]).T
        rows = jnp.where(first, mixed[:SLOTS, :], mixed[SLOTS:, :]).astype(BF16).astype(F32)
        routed[:, cols] = dot(hot[...], (rows * factor).astype(BF16)).astype(BF16)
        both = ((dq_ours[:, cols] + dq_theirs[:, cols]) * SCALE).T
        rows = jnp.where(first, both[:SLOTS, :], both[SLOTS:, :]).astype(BF16)
        d_queries[:, cols] = dot(hot[...], rows).astype(BF16)


def merge_kernel(grads, received, out):
    out[...] = (grads[...] + received[...].astype(F32)).astype(BF16)


def add_kernel(a, b, out):
    out[...] = a[...] + b[...]


def router_kernel(live, d_gate, d_gate_other, gate, t_rows, out):
    value = gate[...]
    d_logit = (d_gate[...] + d_gate_other[...]) * value * (1.0 - value)
    d_logit = own_column(jnp.where(live[...] > 0.0, d_logit, 0.0))
    terms = t_rows[...].astype(F32) * d_logit
    sums = jnp.sum(terms, axis=0, keepdims=True)
    width = out.shape[1]
    out[...] = jnp.zeros_like(out)
    for r in range(sums.shape[1] // width):
        out[r : r + 1, :] = sums[:, r * width : (r + 1) * width]


def put_sum(ref, at, total):
    high = total.astype(BF16)
    ref[at : at + TILE, :] = jnp.concatenate(
        [high.astype(F32), total - high.astype(F32)], axis=0
    ).astype(BF16)


def get_sum(ref, at):
    both = ref[at : at + TILE, :].astype(F32)
    return both[: TILE // 2, :] + both[TILE // 2 :, :]


def sum_x_kernel(own, a, b, r0, r1, keep, router, send):
    size = keep.shape[0]
    router[...] = r0[...] + r1[...]
    for i in range(CHUNK // SLOTS):
        at = slice(i * SLOTS, (i + 1) * SLOTS)
        to = slice(i // 2 * SLOTS, (i // 2 + 1) * SLOTS)
        total = own[at, :] + a[at, :].astype(F32) + b[at, :].astype(F32)
        if i % 2 == 0:
            keep[to, :] = total
        else:
            send[to, :] = total.astype(BF16)
    put_sum(send, size, router[...])


def sum_z_kernel(own, a, r0, r1, r2, dq, keep, router, dq_out, *sends):
    dq_out[...] = dq[...]
    size = keep.shape[0]
    full = own.shape[0]
    total = own[...] + a[:full, :].astype(F32)
    router[...] = r0[...] + get_sum(a, full) + r1[...] + r2[...]
    keep[...] = total[:size, :]
    for i, send in enumerate(sends, 1):
        send[:size, :] = total[i * size : (i + 1) * size, :].astype(BF16)
        put_sum(send, size, router[...])


def last_kernel(hot, own, r0, a, b, c, out, router):
    rows, total = own[...], r0[...]
    for part in (a, b, c):
        rows = rows + part[:SLOTS, :].astype(F32)
        total = total + get_sum(part, SLOTS)
    rows = jnp.concatenate([rows[:, :HEAD_SIZE], rows[:, HEAD_SIZE:]], axis=0).astype(BF16)
    out[...] = dot(hot[...], rows).astype(BF16)
    width = total.shape[1]
    for r in range(router.shape[0] // width):
        router[pl.ds(r * width, width)] = total[r, :]


def on_device(tokens, router_weight, queries, keys_values, routed_grad, chosen, counts):
    count = tokens.shape[0]
    width = queries.shape[1]
    lanes = width // HEAD_SIZE * PAIR
    features = tokens.shape[1]
    pair_width = 2 * HEAD_SIZE

    own_rows = call(
        pick_pairs_kernel,
        shape((SLOTS, pair_width), BF16),
        chosen,
        keys_values.reshape(2 * count, HEAD_SIZE),
        us=0.6,
    )

    pair_row = shape((1, PAIR), F32)
    two = call(
        join_kernel, shape((2 * SLOTS, pair_width), BF16), own_rows, move(own_rows, flip_z)
    )
    live, hot, both_hot, *biases = call(
        masks_kernel,
        (
            pair_row,
            shape((count, SLOTS), BF16),
            shape((2 * count, PAIR), BF16),
            *[shape((CHUNK, PAIR), F32)] * NX,
        ),
        counts,
        chosen,
        specs=[SMEM, VMEM],
        after=(own_rows,),
        us=1.0,
    )
    neighbours = [move(two, by_z(k)) for k in (2, 4, 6)]
    qg_rows, t_rows, logit = call(
        pick_rows_kernel,
        (shape((SLOTS, 2 * width), BF16), shape((SLOTS, features), BF16), pair_row),
        chosen,
        queries,
        routed_grad,
        tokens,
        router_weight.reshape(1, features),
        after=(two, live),
        us=0.6,
    )
    turned, stacked = shape((HEAD_SIZE, lanes), BF16), shape((lanes, HEAD_SIZE), BF16)
    qt, qs, gt = call(
        prepare_kernel,
        (turned, stacked, turned),
        qg_rows,
        move(qg_rows, flip_core),
        us=0.25,
    )
    logit = call(add_kernel, pair_row, logit, flip_tp(logit, 1))
    chunk, logit = call(
        join_sum_kernel,
        (shape((CHUNK, pair_width), BF16), pair_row),
        logit,
        move(logit, flip_core),
        two,
        *neighbours,
    )
    chunks = [chunk] + [move(chunk, by_x(k)) for k in (1, 2, 3)]

    acc_shape, stats_shape = shape((HEAD_SIZE, lanes), F32), shape((8, lanes), F32)
    state = ()
    for k in range(NX):
        extra = ()
        if k == NX - 1:
            gate, dt, ds = call(
                gate_kernel,
                (pair_row, turned, stacked),
                live,
                logit,
                flip_tp(logit, 2),
                gt,
                after=(state[1],),
                us=0.7,
            )
            extra = (dt, gt)
        state = call(
            functools.partial(forward_kernel, k, k == NX - 1),
            (acc_shape, stats_shape),
            biases[k],
            chunks[k],
            qt,
            *extra,
            *state,
            us=0.3,
        )
    acc, stats = state
    stats_other = move(stats, flip_core)
    acc_other = move(acc, flip_core)

    sums = shape((TILE // 2, pair_width), F32)
    part = call(gate_part_kernel, pair_row, stats, stats_other)

    state, order = (), (2, 3, 1, 0)
    for k in order:
        extra, more, after = (), (), ()
        if k == order[1]:
            extra, more = (part, flip_tp(part, 1)), (pair_row,)
        if k == 0:
            after = (router, acc_other, far)
        grad, *state = call(
            functools.partial(backward_kernel, k, order.index(k)),
            (shape((CHUNK, pair_width), F32 if k < 2 else BF16), acc_shape, *more),
            biases[k],
            chunks[k],
            qt,
            qs,
            dt,
            ds,
            stats,
            stats_other,
            *extra,
            *state,
            after=after,
            us=2.3,
        )
        if k == 2:
            handed = move(grad, down_x(2))
        if k == 3:
            part = state.pop()
            far = move(grad, last_to_first)
        if k == 1:
            near = call(merge_kernel, shape((CHUNK, pair_width), BF16), grad, handed, us=0.15)
            router = call(
                router_kernel,
                sums,
                live,
                part,
                flip_tp(part, 2),
                gate,
                t_rows,
                after=(near,),
                us=0.15,
            )
            near = move(near, down_x(1))
            router = call(add_kernel, sums, router, move(router, flip_x(1)))
    dq = state[0]

    half = CHUNK // 2
    keep, router, send = call(
        sum_x_kernel,
        (
            shape((half, pair_width), F32),
            sums,
            shape((half + TILE, pair_width), BF16),
        ),
        grad,
        near,
        far,
        router,
        move(router, flip_x(2)),
        us=0.12,
    )
    keep, router, dq, *sends = call(
        sum_z_kernel,
        (shape((SLOTS, pair_width), F32), sums, acc_shape)
        + (shape((SLOTS + TILE, pair_width), BF16),) * 3,
        keep,
        move(send, flip_z),
        router,
        move(router, flip_core),
        move(router, flip_both),
        dq,
    )
    routed, d_queries, ready = call(
        rows_kernel,
        (shape((count, width), BF16), shape((count, width), BF16), pair_row),
        hot,
        stats,
        stats_other,
        acc,
        acc_other,
        gate,
        dq,
        move(dq, flip_core),
        us=0.1,
    )
    pair_grads, router_grad = call(
        last_kernel,
        (shape((2 * count, HEAD_SIZE), BF16), shape((features,), F32)),
        both_hot,
        keep,
        router,
        *[move(sends[i], by_z(-k)) for i, k in enumerate((2, 4, 6))],
        after=(ready,),
        us=1.4,
    )
    return routed, d_queries, pair_grads.reshape(keys_values.shape), router_grad


def solution(mesh):
    placed = (
        P("ctx", "tp"),
        P("tp"),
        P("ctx", "tp"),
        P("ctx", None, "tp"),
        P("ctx", "tp"),
        P("ctx", None),
        P(),
    )
    return jax.shard_map(
        on_device,
        mesh=mesh,
        in_specs=placed,
        out_specs=(P("ctx", "tp"), P("ctx", "tp"), P("ctx", None, "tp"), P("tp")),
        check_vma=False,
    )
```
